256 devices in a mesh: replica: 4 (over x), section: 16 (over z_hi, y, core), tensor: 4 (over z_lo).
Axes of the slice: x: 4, y: 4, z: 8 (z_hi: 2, z_lo: 4; z = z_hi * 4 + z_lo), core: 2. Of those that a mesh axis runs over, the one named last changes fastest.
Arguments:
- enc_hidden: bfloat16 [4, 512, 4096], P('replica', ('section', 'tensor')), may hold values from -6 to 6
- enc_gain: bfloat16 [4, 4096], P('replica'), may hold values from 0.5 to 1.5
- key_weight: bfloat16 [4, 16, 4096, 2048], P('replica', 'section', None, 'tensor'), may hold values from -0.09375 to 0.09375
- value_weight: bfloat16 [4, 16, 4096, 2048], P('replica', 'section', None, 'tensor'), may hold values from -0.09375 to 0.09375
- queries: bfloat16 [4, 16, 256, 2048], P('replica', 'section', None, 'tensor'), may hold values from -360 to 360
- cotangent: bfloat16 [4, 16, 256, 2048], P('replica', 'section', None, 'tensor'), may hold values from -24 to 24
- enc_len: int32 [4], P('replica'), may hold values from 128 to 512, as said below
- dec_len: int32 [4], P('replica'), may hold values from 64 to 256, as said below
Outputs:
- d_queries: bfloat16 [4, 16, 256, 2048], P('replica', 'section', None, 'tensor')
- d_key_weight: bfloat16 [16, 4096, 2048], P('section', 'replica', 'tensor')
- d_value_weight: bfloat16 [16, 4096, 2048], P('section', 'replica', 'tensor')
- hidden_state_gradient: bfloat16 [4, 512, 4096], P('replica', ('section', 'tensor'))
- d_gain: float32 [4096], replicated
The draws below stay inside these ranges and needn't reach their ends.
Inputs may be any that keep to these rules, and one draw needn't show every extreme that they name: `enc_len`: one replica has all 512 positions, another 512 // 4. `dec_len`: one replica has all 256 tokens, another 256 // 4.
All inputs are finite; a program needn't handle non-finite values.
Results may differ from the reference program's by a relative error of at most 0.017.
The reference program's roundings to bfloat16 on the way count: a program that leaves them out, or rounds other values in their place, can miss the bound.
Values may be sent and summed in bfloat16 or wider, within the bound.
A program may use at most 128 MiB of HBM per device.

```python
import jax
import jax.numpy as jnp
from jax import lax

D = 4096
HEADS = 8
HD = 256
DEC_TOK = 256
TOK_ENC = 512
N_REPLICA = 4
N_SECTION = 16


def draw_lengths(key, total):
    order = jax.random.permutation(jax.random.fold_in(key, 1), N_REPLICA)
    base = jax.random.randint(jax.random.fold_in(key, 2), (N_REPLICA,), total // 4, total + 1)
    base = base.at[order[0]].set(total)
    base = base.at[order[1]].set(total // 4)
    return base.astype(jnp.int32)


def draw_enc_len(key, part):
    key = jax.random.fold_in(key, 11)
    return draw_lengths(key, TOK_ENC)


def draw_dec_len(key, part):
    key = jax.random.fold_in(key, 12)
    return draw_lengths(key, DEC_TOK)


def draw_queries(key, part):
    key = jax.random.fold_in(key, 13)
    shape = (N_REPLICA, N_SECTION, DEC_TOK, HEADS * HD)
    base = jnp.clip(jax.random.normal(jax.random.fold_in(key, 1), shape, jnp.float32), -6.0, 6.0)
    return base.astype(jnp.bfloat16)


def steps_of(key, shape, cuts, smallest, largest):
    level = 1.0
    for position, shards_of in cuts:
        steps = jax.random.uniform(jax.random.fold_in(jax.random.fold_in(key, 6), position), (shards_of,), jnp.float32, smallest / len(cuts), largest / len(cuts))
        level = level * jnp.repeat(jnp.exp(steps), shape[position] // shards_of).reshape((-1,) + (1,) * (len(shape) - 1 - position))
    return level


def centred(own_key, dims, width, reach, pieces=(), kind=jnp.bfloat16):
    drawn = width * jax.random.normal(own_key, dims, jnp.float32)
    if pieces:
        drawn = drawn * steps_of(own_key, dims, pieces, -0.22, 0.18)
    return jnp.clip(drawn, -reach, reach).astype(kind)


def setup_inputs(seed: int = 0) -> dict:
    splits = jax.random.split(jax.random.key(seed), 9)
    return {
        "enc_hidden": centred(splits[0], (N_REPLICA, TOK_ENC, D), 1.0, 6.0, ((0, 4), (1, 64))),
        "enc_gain": jnp.clip(1.0 + 0.1 * jax.random.normal(splits[1], (N_REPLICA, D), jnp.float32), 0.5, 1.5).astype(jnp.bfloat16),
        "key_weight": centred(splits[2], (N_REPLICA, N_SECTION, D, HEADS * HD), D ** -0.5, 0.09375, ((0, 4), (1, 16), (3, 4))),
        "value_weight": centred(splits[3], (N_REPLICA, N_SECTION, D, HEADS * HD), D ** -0.5, 0.09375, ((0, 4), (1, 16), (3, 4))),
        "queries": draw_queries(jax.random.fold_in(splits[8], 71), 0),
        "cotangent": centred(splits[5], (N_REPLICA, N_SECTION, DEC_TOK, HEADS * HD), 4.0, 24.0, ((0, 4), (1, 16), (3, 4))),
        "enc_len": draw_enc_len(jax.random.fold_in(splits[8], 71), 0),
        "dec_len": draw_dec_len(jax.random.fold_in(splits[8], 71), 0),
    }


def attend_back(query_rows, grad_rows, key_rows, value_rows, enc_count, dec_count):
    scale = HD ** (-0.5)
    query_heads = query_rows.reshape(DEC_TOK, HEADS, HD).astype(jnp.float32)
    key_heads = key_rows.reshape(TOK_ENC, HEADS, HD).astype(jnp.float32)
    value_heads = value_rows.reshape(TOK_ENC, HEADS, HD).astype(jnp.float32)
    keep = (jnp.arange(TOK_ENC) < enc_count)[None, None, :]
    scores = jnp.einsum('qhd,khd->hqk', query_heads, key_heads) * scale
    scores = jnp.where(keep, scores, -1e+30)
    top = lax.optimization_barrier(jnp.max(scores, axis=-1, keepdims=True))
    expo = jnp.where(keep, jnp.exp(scores - top), 0.0)
    probs = expo / lax.optimization_barrier(jnp.sum(expo, axis=-1, keepdims=True))
    live = (jnp.arange(DEC_TOK) < dec_count)[:, None]
    grad_in = jnp.where(live, grad_rows, jnp.zeros_like(grad_rows))
    grad_heads = grad_in.reshape(DEC_TOK, HEADS, HD).astype(jnp.float32)
    dprob = jnp.einsum('qhd,khd->hqk', grad_heads, value_heads)
    dscore = probs * (dprob - lax.optimization_barrier(jnp.sum(probs * dprob, axis=-1, keepdims=True)))
    dscore_b = lax.optimization_barrier(dscore.astype(jnp.bfloat16)).astype(jnp.float32)
    probs_b = lax.optimization_barrier(probs.astype(jnp.bfloat16)).astype(jnp.float32)
    d_query = (jnp.einsum('hqk,khd->qhd', dscore_b, key_heads) * scale).reshape(DEC_TOK, HEADS * HD)
    d_key = (jnp.einsum('hqk,qhd->khd', dscore_b, query_heads) * scale).reshape(TOK_ENC, HEADS * HD)
    d_value = jnp.einsum('hqk,qhd->khd', probs_b, grad_heads).reshape(TOK_ENC, HEADS * HD)
    return (d_query.astype(jnp.bfloat16), d_key.astype(jnp.bfloat16), d_value.astype(jnp.bfloat16))

def reference(enc_hidden, enc_gain, key_weight, value_weight, queries, cotangent, enc_len, dec_len):
    query_grads = []
    hidden_grads = []
    total_k = jnp.zeros((N_SECTION, D, HEADS * HD), jnp.float32)
    total_v = jnp.zeros((N_SECTION, D, HEADS * HD), jnp.float32)
    gain_gradient_total = jnp.zeros((D,), jnp.float32)
    for rep in range(N_REPLICA):
        encoder_hidden_state = enc_hidden[rep].astype(jnp.float32)
        root_mean_square = jnp.sqrt(lax.optimization_barrier(jnp.mean(encoder_hidden_state * encoder_hidden_state, axis=-1, keepdims=True)) + 1e-06)
        unit_normalized_input = encoder_hidden_state / root_mean_square
        norm_gain_vector = enc_gain[rep].astype(jnp.float32)
        normalized_hidden = (unit_normalized_input * norm_gain_vector).astype(jnp.bfloat16)

        def layer(carry, inputs):
            w_key, w_value, query_rows, grad_rows = inputs
            key_rows = jnp.dot(normalized_hidden, w_key, preferred_element_type=jnp.float32).astype(jnp.bfloat16)
            value_rows = jnp.dot(normalized_hidden, w_value, preferred_element_type=jnp.float32).astype(jnp.bfloat16)
            d_query, d_key, d_value = attend_back(query_rows, grad_rows, key_rows, value_rows, enc_len[rep], dec_len[rep])
            grad_k = jnp.dot(normalized_hidden.T, d_key, preferred_element_type=jnp.float32).astype(jnp.bfloat16)
            grad_v = jnp.dot(normalized_hidden.T, d_value, preferred_element_type=jnp.float32).astype(jnp.bfloat16)
            back = jnp.dot(d_key, w_key.T, preferred_element_type=jnp.float32)
            back = back + jnp.dot(d_value, w_value.T, preferred_element_type=jnp.float32)
            return (carry + back, (d_query, grad_k, grad_v))
        start = jnp.zeros((TOK_ENC, D), jnp.float32)
        normalized_gradient, (d_query, grad_k, grad_v) = lax.scan(layer, start, (key_weight[rep], value_weight[rep], queries[rep], cotangent[rep]))
        query_grads.append(d_query)
        total_k = total_k + grad_k.astype(jnp.float32)
        total_v = total_v + grad_v.astype(jnp.float32)
        gain_gradient_total = gain_gradient_total + lax.optimization_barrier(jnp.sum(normalized_gradient * unit_normalized_input, axis=0))
        scaled_gradient = norm_gain_vector * normalized_gradient
        hidden_state_gradient = (scaled_gradient - unit_normalized_input * lax.optimization_barrier(jnp.mean(scaled_gradient * unit_normalized_input, axis=-1, keepdims=True))) / root_mean_square
        hidden_grads.append(hidden_state_gradient.astype(jnp.bfloat16))
    d_key_weight = (total_k / N_REPLICA).astype(jnp.bfloat16)
    d_value_weight = (total_v / N_REPLICA).astype(jnp.bfloat16)
    return (jnp.stack(query_grads), d_key_weight, d_value_weight, jnp.stack(hidden_grads), gain_gradient_total / N_REPLICA)
```

```python
import jax
import jax.numpy as jnp
from jax import lax
from jax.experimental import pallas as pl
from jax.experimental.pallas import tpu as pltpu
from jax.sharding import PartitionSpec as P

MESH = pl.DeviceIdType.MESH
F32 = jnp.float32
BF16 = jnp.bfloat16
D = 4096
ROWS = 512
DEC = 256
HD = 256
WID = 512
NX, NY, NZ = 4, 4, 8
QC = D // 4
EC = QC // 4
NSEM = 224


def dot(a, b, ca=1, cb=0):
    return lax.dot_general(a, b, (((ca,), (cb,)), ((), ())), preferred_element_type=F32)


def kernel(
    hid_ref, gain_ref, kw_ref, vw_ref, q_ref, ct_ref, elen_ref, dlen_ref,
    dq_ref, dwk_ref, dwv_ref, hg_ref, dg_ref,
    wk, wv, wsem, n32, x32, own16, G, E, acc, keys, vals, probs, grad, dsc, Dv, Dk,
    Ts, Tr, To, ry, rz, sy, sz, fin, dn, accv, acck,
    gp, gr, gz, gyx, gf, ssem, rsem,
):
    x = lax.axis_index("replica")
    sec = lax.axis_index("section")
    zlo = lax.axis_index("tensor")
    c = lax.rem(sec, 2)
    y = lax.rem(lax.div(sec, 2), NY)
    z = lax.div(sec, 2 * NY) * 4 + zlo
    sib = 1 - c

    def dev(dx=0, dy=0, dz=0, core=None):
        xx = lax.rem(x + dx + NX, NX)
        yy = lax.rem(y + dy + NY, NY)
        zz = lax.rem(z + dz + NZ, NZ)
        cc = c if core is None else core
        return (xx, (lax.div(zz, 4) * NY + yy) * 2 + cc, lax.rem(zz, 4))

    def yo(d):
        return lax.rem(y + d + NY, NY)

    def zo(d):
        return lax.rem(z + d + NZ, NZ)

    sibling = dev(core=sib)
    count = [0]
    sends = []

    def put(src, dst, to):
        i = count[0]
        count[0] += 1
        cp = pltpu.make_async_remote_copy(
            src_ref=src, dst_ref=dst, send_sem=ssem.at[i], recv_sem=rsem.at[i],
            device_id=to, device_id_type=MESH,
        )
        cp.start()
        sends.append(cp)
        return i

    def got(i, region):
        pltpu.make_async_remote_copy(
            src_ref=region, dst_ref=region, send_sem=ssem.at[i], recv_sem=rsem.at[i],
            device_id=sibling, device_id_type=MESH,
        ).wait_recv()

    background = []

    def poll(n=1):
        for _ in range(n):
            for g in list(background):
                if next(g, "end") == "end":
                    background.remove(g)

    def drain():
        while background:
            poll()

    wcopies = [
        pltpu.make_async_copy(kw_ref, wk, wsem.at[0]),
        pltpu.make_async_copy(vw_ref, wv, wsem.at[1]),
    ]
    for w in wcopies:
        w.start()

    partners = [sibling]
    partners += [dev(dz=d) for d in range(1, NZ)]
    partners += [dev(dx=a, dy=b) for a in range(NX) for b in range(NY) if (a, b) != (0, 0)]
    barrier = pltpu.get_barrier_semaphore()
    for p in partners:
        pl.semaphore_signal(barrier, inc=1, device_id=p, device_id_type=MESH)

    hid = hid_ref[...].astype(F32)
    gain = gain_ref[...].astype(F32)
    rms = jnp.sqrt(jnp.mean(hid * hid, axis=-1, keepdims=True) + 1e-06)
    xhat = hid / rms
    n32[...] = (xhat * gain).astype(BF16).astype(F32)
    pl.semaphore_wait(barrier, len(partners))

    i = put(n32, x32, sibling)
    got(i, x32)
    first = jnp.where(c == 0, n32[...], x32[...])
    second = jnp.where(c == 0, x32[...], n32[...])
    chip = jnp.concatenate([first, second], axis=0).astype(BF16)
    for q in range(4):
        own16[q] = chip[:, q * QC:(q + 1) * QC]
    G[2 * c, y, z] = own16[2 * c]
    G[2 * c + 1, y, z] = own16[2 * c + 1]

    def gather8(full, half, landed):
        a = put(full(z), full(z), dev(dz=1))
        b = put(full(z), full(z), dev(dz=-1))
        for k in (1, 2, 3):
            yield
            left, right = zo(-k), zo(k)
            got(a, full(left))
            if k < 3:
                a = put(full(left), full(left), dev(dz=1))
            else:
                a = put(half(left, 0), half(left, 0), dev(dz=1))
            got(b, full(right))
            if k < 3:
                b = put(full(right), full(right), dev(dz=-1))
            else:
                b = put(half(right, 1), half(right, 1), dev(dz=-1))
            landed(left)
            landed(right)
        yield
        far = zo(4)
        got(a, half(far, 0))
        got(b, half(far, 1))
        landed(far)

    def gather4(half, landed, mine, back, ahead, dst):
        a0 = put(half(mine, 0), half(mine, 0), dst(1))
        b1 = put(half(mine, 1), half(mine, 1), dst(-1))
        a1 = put(half(mine, 1), half(mine, 1), dst(1))
        b0 = put(half(mine, 0), half(mine, 0), dst(-1))
        yield
        got(a0, half(back(1), 0))
        f0 = put(half(back(1), 0), half(back(1), 0), dst(1))
        got(b1, half(ahead(1), 1))
        f1 = put(half(ahead(1), 1), half(ahead(1), 1), dst(-1))
        yield
        got(a1, half(back(1), 1))
        landed(back(1))
        got(b0, half(ahead(1), 0))
        landed(ahead(1))
        yield
        got(f0, half(ahead(2), 0))
        got(f1, half(ahead(2), 1))
        landed(ahead(2))

    def plane_gather(buf, lead, width, arrivals):
        pre = (slice(None),) * lead
        hw = width // 2
        lanes = (pl.ds(0, hw), pl.ds(hw, hw))

        def forward(region):
            i = put(region(c), region(c), sibling)
            arrivals.append((i, region(sib)))

        def first_z():
            def full(zz):
                return buf.at[(2 * c,) + pre + (y, zz)]

            def half(zz, h):
                return buf.at[(2 * c,) + pre + (y, zz, slice(None), lanes[h])]

            yield from gather8(full, half, lambda zz: None)
            forward(lambda cc: buf.at[(2 * cc,) + pre + (y,)])

            def yhalf(yy, h):
                return buf.at[(2 * c,) + pre + (yy, pl.ds(4 * h, 4))]

            def landed(yy):
                forward(lambda cc: buf.at[(2 * cc,) + pre + (yy,)])

            yield from gather4(
                yhalf, landed, y, lambda d: yo(-d), yo, lambda d: dev(dy=d)
            )

        def first_y():
            def half(yy, h):
                return buf.at[(2 * c + 1,) + pre + (yy, z, slice(None), lanes[h])]

            yield from gather4(
                half, lambda yy: None, y, lambda d: yo(-d), yo, lambda d: dev(dy=d)
            )

            def full(zz):
                return buf.at[(2 * c + 1,) + pre + (slice(None), zz)]

            def zhalf(zz, h):
                return buf.at[(2 * c + 1,) + pre + (pl.ds(2 * h, 2), zz)]

            def landed(zz):
                forward(lambda cc: buf.at[(2 * cc + 1,) + pre + (slice(None), zz)])

            landed(z)
            yield from gather8(full, zhalf, landed)

        return [first_z(), first_y()]

    g_arrivals = []
    background += plane_gather(G, 0, QC, g_arrivals)
    poll()
    extra = []
    for k in (1, 2, 3):
        to = lax.rem(x - k + NX, NX)
        for h in range(2):
            lane = pl.multiple_of((2 * c + h) * EC, EC)
            src = own16.at[to, :, pl.ds(lane, EC)]
            slot = E.at[2 * c + h, k - 1, y, z]
            extra.append((put(src, slot, dev(dx=-k)), slot))
    drain()

    for i, region in extra:
        got(i, region)
    e_arrivals = []
    background += plane_gather(E, 1, EC, e_arrivals)
    poll()

    def project(w, out, first):
        for j in range(4):
            if first and j == 2:
                for i, region in g_arrivals:
                    got(i, region)
            q = lax.rem(2 * c + j, 4)
            g = G[q].reshape(ROWS, QC)
            part = dot(g, w[pl.ds(pl.multiple_of(q * QC, QC), QC), :])
            if j == 0:
                acc[...] = part
            elif j < 3:
                acc[...] += part
            else:
                out[...] = (acc[...] + part).astype(BF16)
            if j % 2 == 1:
                poll()

    scale = HD ** (-0.5)
    wcopies[0].wait()
    project(wk, keys, True)

    row = lax.broadcasted_iota(jnp.int32, (ROWS, 1), 0)
    inner = row & 7
    rc = (row >> 3) & 1
    rz_ = (row >> 4) & 7
    ry_ = row >> 7
    pos = ((((rz_ >> 2) * NY + ry_) * 2 + rc) * 4 + (rz_ & 3)) * 8 + inner
    keep = pos < elen_ref[0]
    live = lax.broadcasted_iota(jnp.int32, (DEC, 1), 0) < dlen_ref[0]
    grad[...] = jnp.where(live, ct_ref[...], jnp.zeros((DEC, WID), BF16))
    for h in range(2):
        cols = slice(h * HD, (h + 1) * HD)
        s = dot(keys[:, cols], q_ref[:, cols], 1, 1) * scale
        s = jnp.where(keep, s, -1e30)
        top = jnp.max(s, axis=0, keepdims=True)
        e = jnp.where(keep, jnp.exp(s - top), 0.0)
        p = e / jnp.sum(e, axis=0, keepdims=True)
        probs[h] = p
        Dv[0, :, cols] = dot(p.astype(BF16), grad[:, cols]).astype(BF16)

    def along_x(buf):
        def at(slot, h):
            return buf.at[slot, pl.ds(h * (ROWS // 2), ROWS // 2)]

        a0 = put(at(0, 0), at(3, 0), dev(dx=1))
        b1 = put(at(0, 1), at(1, 1), dev(dx=-1))
        a1 = put(at(0, 1), at(3, 1), dev(dx=1))
        b0 = put(at(0, 0), at(1, 0), dev(dx=-1))
        yield
        got(a0, at(3, 0))
        f0 = put(at(3, 0), at(2, 0), dev(dx=1))
        got(b1, at(1, 1))
        f1 = put(at(1, 1), at(2, 1), dev(dx=-1))
        yield
        got(a1, at(3, 1))
        got(b0, at(1, 0))
        yield
        got(f0, at(2, 0))
        got(f1, at(2, 1))

    xv = along_x(Dv)
    next(xv)
    wcopies[1].wait()
    project(wv, vals, False)
    for h in range(2):
        cols = slice(h * HD, (h + 1) * HD)
        dp = dot(vals[:, cols], grad[:, cols], 1, 1)
        p = probs[h]
        ds = (p * (dp - jnp.sum(p * dp, axis=0, keepdims=True))).astype(BF16)
        dsc[h] = ds
        Dk[0, :, cols] = (dot(ds, q_ref[:, cols]) * scale).astype(BF16)
    xk = along_x(Dk)
    next(xk)

    t_in = []
    for j in range(4):
        q = lax.rem(2 * sib + j, 4)
        w = pl.ds(pl.multiple_of(q * QC, QC), QC)
        t = dot(Dk[0], wk[w, :], 1, 1) + dot(Dv[0], wv[w, :], 1, 1)
        if j < 2:
            Ts[j] = t.astype(BF16).reshape(NY, NZ, 16, QC)
            t_in.append(put(Ts.at[j], Tr.at[j], sibling))
        else:
            To[j - 2] = t.reshape(NY, NZ, 16, QC)
        poll()
    next(xv, None)

    def sum4(own, stage, land, base, dst, put_result, mine, off):
        def send(slot, value, to):
            stage[base + slot] = value.astype(BF16)
            return put(stage.at[base + slot], land.at[base + slot], to)

        a0 = send(0, own(off(2), 0), dst(1))
        b1 = send(1, own(off(2), 1), dst(-1))
        a1 = send(2, own(off(1), 1), dst(1))
        b0 = send(3, own(off(-1), 0), dst(-1))
        yield
        got(a0, land.at[base])
        f0 = send(4, own(off(1), 0) + land[base].astype(F32), dst(1))
        got(b1, land.at[base + 1])
        f1 = send(5, own(off(-1), 1) + land[base + 1].astype(F32), dst(-1))
        yield
        got(a1, land.at[base + 2])
        got(b0, land.at[base + 3])
        yield
        got(f0, land.at[base + 4])
        got(f1, land.at[base + 5])
        put_result(0, own(mine, 0) + land[base + 3].astype(F32) + land[base + 4].astype(F32))
        put_result(1, own(mine, 1) + land[base + 2].astype(F32) + land[base + 5].astype(F32))

    def sum8(own, stage, land, put_result):
        stage[0, 0] = own(zo(4), 0).astype(BF16)
        a = put(stage.at[0, 0], land.at[0, 0], dev(dz=1))
        stage[4, 1] = own(zo(4), 1).astype(BF16)
        b = put(stage.at[4, 1], land.at[4, 1], dev(dz=-1))
        for s, k in ((1, 3), (2, 2), (3, 1)):
            yield
            if s == 1:
                got(a, land.at[0, 0])
            else:
                got(a, land.at[s - 1])
            for h in range(2):
                v = own(zo(k), h)
                if s > 1 or h == 0:
                    v = v + land[s - 1, h].astype(F32)
                stage[s, h] = v.astype(BF16)
            a = put(stage.at[s], land.at[s], dev(dz=1))
            if s == 1:
                got(b, land.at[4, 1])
            else:
                got(b, land.at[3 + s])
            for h in range(2):
                v = own(zo(-k), h)
                if s > 1 or h == 1:
                    v = v + land[3 + s, h].astype(F32)
                stage[4 + s, h] = v.astype(BF16)
            b = put(stage.at[4 + s], land.at[4 + s], dev(dz=-1))
        yield
        got(a, land.at[3])
        got(b, land.at[7])
        for h in range(2):
            put_result(h, own(z, h) + land[3, h].astype(F32) + land[7, h].astype(F32))

    hq = QC // 2
    lanes = (slice(0, hq), slice(hq, QC))

    def sum_y_first():
        got(t_in[0], Tr.at[0])
        To[0] += Tr[0].astype(F32)

        def own(yy, h):
            return To[0, yy, 4 * h:4 * h + 4]

        def result(h, v):
            To[0, y, 4 * h:4 * h + 4] = v

        yield from sum4(own, sy[0], ry[0], 0, lambda d: dev(dy=d), result, y, yo)

        def own2(zz, h):
            return To[0, y, zz, :, lanes[h]]

        def result2(h, v):
            fin[0, :, :, lanes[h]] = v.reshape(2, 8, hq)

        yield from sum8(own2, sz[0], rz[0], result2)

    def sum_z_first():
        got(t_in[1], Tr.at[1])
        To[1] += Tr[1].astype(F32)

        def own(zz, h):
            return To[1, 2 * h:2 * h + 2, zz]

        def result(h, v):
            To[1, 2 * h:2 * h + 2, z] = v

        yield from sum8(own, sz[1], rz[1], result)

        def own2(yy, h):
            return To[1, yy, z, :, lanes[h]]

        def result2(h, v):
            fin[1, :, :, lanes[h]] = v.reshape(2, 8, hq)

        yield from sum4(own2, sy[1], ry[1], 0, lambda d: dev(dy=d), result2, y, yo)

    drain()
    for i, region in e_arrivals:
        got(i, region)

    def weight_part(buf, total, out, k):
        for q in range(4):
            r = slice(q * EC, (q + 1) * EC)
            if k == 0:
                total[r, :] = dot(G[x].reshape(ROWS, QC)[:, r], buf[0], 0, 0)
            else:
                part = dot(E[q, k - 1].reshape(ROWS, EC), buf[k], 0, 0)
                if k == 2:
                    out[r, :] = ((total[r, :] + part) / NX).astype(BF16)
                else:
                    total[r, :] += part

    def queries():
        for h in range(2):
            cols = slice(h * HD, (h + 1) * HD)
            dq_ref[:, cols] = (dot(dsc[h], keys[:, cols], 0, 0) * scale).astype(BF16)

    background += [sum_y_first(), sum_z_first()]
    poll()
    queries()
    poll()
    weight_part(Dv, accv, dwv_ref, 0)
    poll()
    weight_part(Dk, acck, dwk_ref, 0)
    poll()
    next(xv, None)
    weight_part(Dv, accv, dwv_ref, 1)
    poll()
    next(xv, None)
    weight_part(Dv, accv, dwv_ref, 3)
    poll()
    drain()

    i = put(fin.at[:, sib], dn, sibling)
    got(i, dn)
    own_half = jnp.concatenate([fin[0, c], fin[1, c]], axis=1)
    other = jnp.concatenate([dn[0], dn[1]], axis=1)
    dnorm = jnp.concatenate(
        [jnp.where(c == 0, own_half, other), jnp.where(c == 0, other, own_half)], axis=1
    )
    terms = jnp.sum(dnorm * xhat, axis=0, keepdims=True)
    for j in range(8):
        for h in range(2):
            lo = j * 512 + h * 256
            gp[h, j:j + 1, :] = terms[:, lo:lo + 256]
    i1 = put(gp.at[sib], gr, sibling)
    scaled = gain * dnorm
    hg = (scaled - xhat * jnp.mean(scaled * xhat, axis=-1, keepdims=True)) / rms
    hg_ref[...] = hg.astype(BF16)
    got(i1, gr)
    gz[z] = gp[c] + gr[...]
    idx = [put(gz.at[z], gz.at[z], dev(dz=d)) for d in range(1, NZ)]
    next(xk, None)
    for d, i in zip(range(1, NZ), idx):
        got(i, gz.at[zo(-d)])
    slot = y * NX + x
    gyx[slot] = jnp.sum(gz[...], axis=0)
    idx = []
    for a in range(NX):
        for b in range(NY):
            if (a, b) != (0, 0):
                i = put(gyx.at[slot], gyx.at[slot], dev(dx=a, dy=b))
                idx.append((i, yo(-b) * NX + lax.rem(x - a + NX, NX)))
    for i, s in idx:
        got(i, gyx.at[s])
    gf[c] = jnp.sum(gyx[...], axis=0) / NX
    i2 = put(gf.at[c], gf.at[c], sibling)

    next(xv, None)
    weight_part(Dv, accv, dwv_ref, 2)
    next(xk, None)
    weight_part(Dk, acck, dwk_ref, 1)
    weight_part(Dk, acck, dwk_ref, 3)
    got(i2, gf.at[sib])
    for j in range(8):
        for h in range(2):
            lo = j * 512 + h * 256
            dg_ref[0:1, lo:lo + 256] = gf[h, j:j + 1, :]
    next(xk, None)
    weight_part(Dk, acck, dwk_ref, 2)
    for cp in sends:
        cp.wait_send()
    assert count[0] <= NSEM, count[0]


def local(enc_hidden, enc_gain, key_weight, value_weight, queries, cotangent, enc_len, dec_len):
    vmem = pl.BlockSpec(memory_space=pltpu.VMEM)
    hbm = pl.BlockSpec(memory_space=pl.ANY)
    smem = pl.BlockSpec(memory_space=pltpu.SMEM)
    v = pltpu.VMEM
    outs = pl.pallas_call(
        kernel,
        out_shape=(
            jax.ShapeDtypeStruct((DEC, WID), BF16),
            jax.ShapeDtypeStruct((QC, WID), BF16),
            jax.ShapeDtypeStruct((QC, WID), BF16),
            jax.ShapeDtypeStruct((8, D), BF16),
            jax.ShapeDtypeStruct((1, D), F32),
        ),
        in_specs=[vmem, vmem, hbm, hbm, vmem, vmem, smem, smem],
        out_specs=(vmem,) * 5,
        scratch_shapes=[
            v((D, WID), BF16),
            v((D, WID), BF16),
            pltpu.SemaphoreType.DMA((2,)),
            v((8, D), F32),
            v((8, D), F32),
            v((4, 16, QC), BF16),
            v((4, NY, NZ, 16, QC), BF16),
            v((4, 3, NY, NZ, 16, EC), BF16),
            v((ROWS, WID), F32),
            v((ROWS, WID), BF16),
            v((ROWS, WID), BF16),
            v((2, ROWS, DEC), F32),
            v((DEC, WID), BF16),
            v((2, ROWS, DEC), BF16),
            v((4, ROWS, WID), BF16),
            v((4, ROWS, WID), BF16),
            v((2, NY, NZ, 16, QC), BF16),
            v((2, NY, NZ, 16, QC), BF16),
            v((2, NY, NZ, 16, QC), F32),
            [v((6, 4, 16, QC), BF16), v((6, 16, QC // 2), BF16)],
            [v((8, 2, 16, QC // 2), BF16), v((8, 2, 2, 16, QC), BF16)],
            [v((6, 4, 16, QC), BF16), v((6, 16, QC // 2), BF16)],
            [v((8, 2, 16, QC // 2), BF16), v((8, 2, 2, 16, QC), BF16)],
            v((2, 2, 8, QC), F32),
            v((2, 8, QC), F32),
            v((QC, WID), F32),
            v((QC, WID), F32),
            v((2, 8, 256), F32),
            v((8, 256), F32),
            v((NZ, 8, 256), F32),
            v((NX * NY, 8, 256), F32),
            v((2, 8, 256), F32),
            pltpu.SemaphoreType.DMA((NSEM,)),
            pltpu.SemaphoreType.DMA((NSEM,)),
        ],
        compiler_params=pltpu.CompilerParams(
            collective_id=0, has_side_effects=True, vmem_limit_bytes=60 * 1024 * 1024
        ),
        cost_estimate=pl.CostEstimate(
            flops=15_000_000_000, bytes_accessed=12_000_000, transcendentals=300_000
        ),
    )(
        enc_hidden[0], enc_gain, key_weight[0, 0], value_weight[0, 0],
        queries[0, 0], cotangent[0, 0], enc_len, dec_len,
    )
    dq, dwk, dwv, hg, dg = outs
    return dq[None, None], dwk[None], dwv[None], hg[None], dg[0]


def solution(mesh):
    placed = (
        P("replica", ("section", "tensor"), None),
        P("replica", None),
        P("replica", "section", None, "tensor"),
        P("replica", "section", None, "tensor"),
        P("replica", "section", None, "tensor"),
        P("replica", "section", None, "tensor"),
        P("replica"),
        P("replica"),
    )
    return jax.shard_map(
        local,
        mesh=mesh,
        in_specs=placed,
        out_specs=(
            P("replica", "section", None, "tensor"),
            P("section", "replica", "tensor"),
            P("section", "replica", "tensor"),
            P("replica", ("section", "tensor"), None),
            P(),
        ),
        check_vma=False,
    )
```

```python
import jax
import jax.numpy as jnp
from jax import lax
from jax.experimental import pallas as pl
from jax.experimental.pallas import tpu as pltpu
from jax.sharding import PartitionSpec as P

MESH = pl.DeviceIdType.MESH
F32 = jnp.float32
BF16 = jnp.bfloat16
D = 4096
ROWS = 512
DEC = 256
HD = 256
WID = 512
NX, NY, NZ = 4, 4, 8
QC = D // 4
EC = QC // 4
NSEM = 96
NSEND = 48


def dot(a, b, ca=1, cb=0):
    return lax.dot_general(a, b, (((ca,), (cb,)), ((), ())), preferred_element_type=F32)


def kernel(
    hid_ref, gain_ref, kw_ref, vw_ref, q_ref, ct_ref, elen_ref, dlen_ref,
    dq_ref, dwk_ref, dwv_ref, hg_ref, dg_ref,
    wk, wv, wsem, n32, x32, G, E, acc, keys, vals, probs, grad, dsc, Dv, Dk,
    Ts, Tr, To, ly, lz, sy, sz, fin, dn, accv, acck,
    gz, gy, gx, gf, ssem, rsem, esend, erecv,
):
    x = lax.axis_index("replica")
    sec = lax.axis_index("section")
    zlo = lax.axis_index("tensor")
    c = lax.rem(sec, 2)
    y = lax.rem(lax.div(sec, 2), NY)
    z = lax.div(sec, 2 * NY) * 4 + zlo
    sib = 1 - c

    def dev(dx=0, dy=0, dz=0, core=None):
        xx = lax.rem(x + dx + NX, NX)
        yy = lax.rem(y + dy + NY, NY)
        zz = lax.rem(z + dz + NZ, NZ)
        cc = c if core is None else core
        return (xx, (lax.div(zz, 4) * NY + yy) * 2 + cc, lax.rem(zz, 4))

    def xo(d):
        return lax.rem(x + d + NX, NX)

    def yo(d):
        return lax.rem(y + d + NY, NY)

    def zo(d):
        return lax.rem(z + d + NZ, NZ)

    sibling = dev(core=sib)
    count = [0]
    sends = {}

    def put(src, dst, to):
        i = count[0]
        count[0] += 1
        s = i % NSEND
        if s in sends:
            sends[s].wait_send()
        cp = pltpu.make_async_remote_copy(
            src_ref=src, dst_ref=dst, send_sem=ssem.at[s], recv_sem=rsem.at[i],
            device_id=to, device_id_type=MESH,
        )
        cp.start()
        sends[s] = cp
        return i

    def got(i, region):
        pltpu.make_async_remote_copy(
            src_ref=region, dst_ref=region, send_sem=ssem.at[0], recv_sem=rsem.at[i],
            device_id=sibling, device_id_type=MESH,
        ).wait_recv()

    background = []

    def poll(n=1):
        for _ in range(n):
            for g in list(background):
                if next(g, "end") == "end":
                    background.remove(g)

    def drain():
        while background:
            poll()

    wcopies = [
        pltpu.make_async_copy(kw_ref, wk, wsem.at[0]),
        pltpu.make_async_copy(vw_ref, wv, wsem.at[1]),
    ]
    for w in wcopies:
        w.start()

    partners = [sibling]
    partners += [dev(dz=d) for d in range(1, NZ)]
    partners += [dev(dy=d) for d in range(1, NY)]
    partners += [dev(dx=d) for d in range(1, NX)]
    barrier = pltpu.get_barrier_semaphore()
    for p in partners:
        pl.semaphore_signal(barrier, inc=1, device_id=p, device_id_type=MESH)

    hid = hid_ref[...].astype(F32)
    gain = gain_ref[...].astype(F32)
    rms = jnp.sqrt(jnp.mean(hid * hid, axis=-1, keepdims=True) + 1e-06)
    xhat = hid / rms
    n32[...] = (xhat * gain).astype(BF16).astype(F32)
    pl.semaphore_wait(barrier, len(partners))

    hc = D // 2
    i = put(n32.at[:, pl.ds(pl.multiple_of(sib * hc, hc), hc)], x32, sibling)
    mine = jnp.where(c == 0, n32[:, :hc], n32[:, hc:])
    got(i, x32)
    other = x32[...]
    chip = jnp.concatenate(
        [jnp.where(c == 0, mine, other), jnp.where(c == 0, other, mine)], axis=0
    ).astype(BF16)
    for j in range(2):
        G[2 * c + j, y, z] = chip[:, j * QC:(j + 1) * QC]

    def ring8(half, landed):
        a = [put(half(z, h), half(z, h), dev(dz=1)) for h in (0, 1)]
        b = [put(half(z, h), half(z, h), dev(dz=-1)) for h in (1, 0)][::-1]
        for k in (1, 2, 3):
            yield
            left, right = zo(-k), zo(k)
            for far in (True, False):
                ha, hb = (0, 1) if far else (1, 0)
                got(a[ha], half(left, ha))
                if k < 3 or far:
                    a[ha] = put(half(left, ha), half(left, ha), dev(dz=1))
                got(b[hb], half(right, hb))
                if k < 3 or far:
                    b[hb] = put(half(right, hb), half(right, hb), dev(dz=-1))
            landed(left)
            landed(right)
        yield
        got(a[0], half(zo(4), 0))
        got(b[1], half(zo(4), 1))
        landed(zo(4))

    arrivals = []

    def forward(region):
        i = put(region(c), region(c), sibling)
        arrivals.append((i, region(sib)))

    def to_replica(j, at):
        q = 2 * c + j

        @pl.when(q != x)
        def _():
            slot = jnp.maximum(lax.rem(x - q + NX, NX) - 1, 0)
            pltpu.make_async_remote_copy(
                src_ref=G.at[(q,) + at], dst_ref=E.at[(slot,) + at],
                send_sem=esend.at[j], recv_sem=erecv.at[slot],
                device_id=dev(dx=q - x), device_id_type=MESH,
            ).start()

    every = slice(None)

    def gather_z_first():
        q = 2 * c
        order = (4, 3, 5, 2, 6, 1, 7)
        idx = [put(G.at[q, y, z], G.at[q, y, z], dev(dz=d)) for d in order]
        yield
        yield
        for d, i in zip(order, idx):
            got(i, G.at[q, y, zo(-d)])
        order = (2, 1, 3)
        idx = [put(G.at[q, y], G.at[q, y], dev(dy=d)) for d in order]
        forward(lambda cc: G.at[2 * cc, y])
        to_replica(0, (y,))
        yield
        yield
        for d, i in zip(order, idx):
            yy = yo(-d)
            got(i, G.at[q, yy])
            forward(lambda cc: G.at[2 * cc, yy])
            to_replica(0, (yy,))

    def gather_y_first():
        q = 2 * c + 1
        order = (2, 1, 3)
        idx = [put(G.at[q, y, z], G.at[q, y, z], dev(dy=d)) for d in order]
        yield
        for d, i in zip(order, idx):
            got(i, G.at[q, yo(-d), z])

        def half(zz, h):
            return G.at[q, pl.ds(2 * h, 2), zz]

        def landed(zz):
            forward(lambda cc: G.at[2 * cc + 1, :, zz])
            to_replica(1, (every, zz))

        first = ring8(half, landed)
        next(first)
        landed(z)
        yield
        yield from first

    background += [gather_y_first(), gather_z_first()]
    drain()

    def project(w, out, first):
        for j in range(4):
            if first and j == 2:
                for i, region in arrivals:
                    got(i, region)
            q = lax.rem(2 * c + j, 4)
            part = dot(G[q].reshape(ROWS, QC), w[pl.ds(pl.multiple_of(q * QC, QC), QC), :])
            if j == 0:
                acc[...] = part
            elif j < 3:
                acc[...] += part
            else:
                out[...] = (acc[...] + part).astype(BF16)

    scale = HD ** (-0.5)
    row = lax.broadcasted_iota(jnp.int32, (ROWS, 1), 0)
    inner = row & 7
    row_c = (row >> 3) & 1
    row_z = (row >> 4) & 7
    row_y = row >> 7
    pos = ((((row_z >> 2) * NY + row_y) * 2 + row_c) * 4 + (row_z & 3)) * 8 + inner
    keep = pos < elen_ref[0]
    live = lax.broadcasted_iota(jnp.int32, (DEC, 1), 0) < dlen_ref[0]
    grad[...] = jnp.where(live, ct_ref[...], jnp.zeros((DEC, WID), BF16))
    wcopies[0].wait()
    project(wk, keys, True)
    for h in range(2):
        cols = slice(h * HD, (h + 1) * HD)
        s = dot(keys[:, cols], q_ref[:, cols], 1, 1) * scale
        s = jnp.where(keep, s, -1e30)
        top = jnp.max(s, axis=0, keepdims=True)
        e = jnp.where(keep, jnp.exp(s - top), 0.0)
        p = e / jnp.sum(e, axis=0, keepdims=True)
        probs[h] = p
        Dv[0, :, cols] = dot(p.astype(BF16), grad[:, cols]).astype(BF16)

    def along_x(buf):
        def at(slot, h):
            return buf.at[slot, pl.ds(h * (ROWS // 2), ROWS // 2)]

        a0 = put(at(0, 0), at(3, 0), dev(dx=1))
        b1 = put(at(0, 1), at(1, 1), dev(dx=-1))
        a1 = put(at(0, 1), at(3, 1), dev(dx=1))
        b0 = put(at(0, 0), at(1, 0), dev(dx=-1))
        yield
        got(a0, at(3, 0))
        f0 = put(at(3, 0), at(2, 0), dev(dx=1))
        got(b1, at(1, 1))
        f1 = put(at(1, 1), at(2, 1), dev(dx=-1))
        yield
        got(a1, at(3, 1))
        got(b0, at(1, 0))
        yield
        got(f0, at(2, 0))
        got(f1, at(2, 1))

    xv = along_x(Dv)
    next(xv)
    wcopies[1].wait()
    project(wv, vals, False)
    for h in range(2):
        cols = slice(h * HD, (h + 1) * HD)
        dp = dot(vals[:, cols], grad[:, cols], 1, 1)
        p = probs[h]
        ds = (p * (dp - jnp.sum(p * dp, axis=0, keepdims=True))).astype(BF16)
        dsc[h] = ds
        Dk[0, :, cols] = (dot(ds, q_ref[:, cols]) * scale).astype(BF16)
    xk = along_x(Dk)
    next(xk)

    def sum_y_first():
        order = (2, 1, 3)
        idx = []
        for d in order:
            sy[0][d - 1] = To[0, yo(d)].astype(BF16)
            idx.append(put(sy[0].at[d - 1], ly[0].at[d - 1], dev(dy=d)))
        yield
        yield
        for d, i in zip(order, idx):
            got(i, ly[0].at[d - 1])
        v = To[0, y]
        for d in range(3):
            v = v + ly[0][d].astype(F32)
        To[0, y] = v
        order = (4, 3, 5, 2, 6, 1, 7)
        idx = []
        for d in order:
            sz[0][d - 1] = To[0, y, zo(d)].astype(BF16)
            idx.append(put(sz[0].at[d - 1], lz[0].at[d - 1], dev(dz=d)))
        yield
        yield
        for d, i in zip(order, idx):
            got(i, lz[0].at[d - 1])
        v = To[0, y, z]
        for d in range(7):
            v = v + lz[0][d].astype(F32)
        fin[0] = v.reshape(2, 8, QC)

    def sum_z_first():
        stage, land = sz[1], lz[1]

        def own(zz, h):
            return To[1, 2 * h:2 * h + 2, zz]

        def send(slot, h, value, to):
            stage[slot, h] = value.astype(BF16)
            return put(stage.at[slot, h], land.at[slot, h], to)

        a, b = [None, None], [None, None]
        a[0] = send(0, 0, own(zo(4), 0), dev(dz=1))
        b[1] = send(4, 1, own(zo(4), 1), dev(dz=-1))
        a[1] = send(1, 1, own(zo(3), 1), dev(dz=1))
        b[0] = send(5, 0, own(zo(-3), 0), dev(dz=-1))
        for s, k in ((1, 3), (2, 2), (3, 1)):
            yield
            for h in ((0, 1) if s > 1 else (0,)):
                got(a[h], land.at[s - 1, h])
                a[h] = send(s, h, own(zo(k), h) + land[s - 1, h].astype(F32), dev(dz=1))
                g = 1 - h
                got(b[g], land.at[3 + s, g])
                b[g] = send(4 + s, g, own(zo(-k), g) + land[3 + s, g].astype(F32), dev(dz=-1))
        yield
        for h in range(2):
            got(a[h], land.at[3, h])
            got(b[h], land.at[7, h])
            To[1, 2 * h:2 * h + 2, z] = (
                own(z, h) + land[3, h].astype(F32) + land[7, h].astype(F32)
            )
        order = (2, 1, 3)
        idx = []
        for d in order:
            sy[1][d - 1] = To[1, yo(d), z].astype(BF16)
            idx.append(put(sy[1].at[d - 1], ly[1].at[d - 1], dev(dy=d)))
        yield
        for d, i in zip(order, idx):
            got(i, ly[1].at[d - 1])
        v = To[1, y, z]
        for d in range(3):
            v = v + ly[1][d].astype(F32)
        fin[1] = v.reshape(2, 8, QC)

    t_in = []
    sums = [sum_y_first(), sum_z_first()]
    for j in range(4):
        q = lax.rem(2 * sib + j, 4)
        w = pl.ds(pl.multiple_of(q * QC, QC), QC)
        t = dot(Dk[0], wk[w, :], 1, 1) + dot(Dv[0], wv[w, :], 1, 1)
        if j < 2:
            Ts[j] = t.astype(BF16).reshape(NY, NZ, 16, QC)
            t_in.append(put(Ts.at[j], Tr.at[j], sibling))
        else:
            got(t_in[j - 2], Tr.at[j - 2])
            To[j - 2] = t.reshape(NY, NZ, 16, QC) + Tr[j - 2].astype(F32)
            next(sums[j - 2])
    next(xv)

    gsel = jnp.where(c == 0, gain[:, :hc], gain[:, hc:])
    for j in range(2):
        prod = To[j].reshape(ROWS, QC) * G[2 * c + j].reshape(ROWS, QC).astype(F32)
        terms = jnp.sum(prod, axis=0, keepdims=True) / gsel[:, j * QC:(j + 1) * QC]
        for r in range(4):
            gz[z, 4 * j + r:4 * j + r + 1, :] = terms[:, r * 256:(r + 1) * 256]

    def sum_gain():
        idx = [(put(gz.at[z], gz.at[z], dev(dz=d)), zo(-d)) for d in range(1, NZ)]
        yield
        for i, s in idx:
            got(i, gz.at[s])
        gy[y] = jnp.sum(gz[...], axis=0)
        idx = [(put(gy.at[y], gy.at[y], dev(dy=d)), yo(-d)) for d in range(1, NY)]
        yield
        for i, s in idx:
            got(i, gy.at[s])
        gx[x] = jnp.sum(gy[...], axis=0)
        idx = [(put(gx.at[x], gx.at[x], dev(dx=d)), xo(-d)) for d in range(1, NX)]
        yield
        for i, s in idx:
            got(i, gx.at[s])
        gf[c] = jnp.sum(gx[...], axis=0) / NX
        i = put(gf.at[c], gf.at[c], sibling)
        yield
        got(i, gf.at[sib])
        for h in range(2):
            for r in range(8):
                lo = h * hc + r * 256
                dg_ref[0:1, lo:lo + 256] = gf[h, r:r + 1, :]

    def weight_part(buf, total, out, k):
        src = G.at[x] if k == 0 else E.at[k - 1]
        for q in range(4):
            r = slice(q * EC, (q + 1) * EC)
            part = dot(src[:, :, :, r].reshape(ROWS, EC), buf[k], 0, 0)
            if k == 0:
                total[r, :] = part
            elif k == 2:
                out[r, :] = ((total[r, :] + part) / NX).astype(BF16)
            else:
                total[r, :] += part

    background += sums + [sum_gain()]
    poll()
    for h in range(2):
        cols = slice(h * HD, (h + 1) * HD)
        dq_ref[:, cols] = (dot(dsc[h], keys[:, cols], 0, 0) * scale).astype(BF16)
    weight_part(Dv, accv, dwv_ref, 0)
    poll()
    weight_part(Dk, acck, dwk_ref, 0)

    owner = lax.div(x, 2)
    handed = []
    for k in range(3):
        def piece(send, recv):
            return pltpu.make_async_remote_copy(
                src_ref=E.at[k], dst_ref=E.at[k], send_sem=esend.at[send],
                recv_sem=erecv.at[recv], device_id=sibling, device_id_type=MESH,
            )

        @pl.when(c == owner)
        def _():
            piece(2 + k, k).wait_recv()
            piece(2 + k, 3 + k).start()

        handed.append(piece(2 + k, 3 + k))
    poll()
    next(xv)
    for cp in handed:
        @pl.when(c != owner)
        def _():
            cp.wait_recv()
    weight_part(Dv, accv, dwv_ref, 1)
    weight_part(Dv, accv, dwv_ref, 3)
    poll()
    next(xk)
    next(xv, None)
    weight_part(Dv, accv, dwv_ref, 2)
    drain()

    i = put(fin.at[:, sib], dn, sibling)
    got(i, dn)
    own_half = jnp.concatenate([fin[0, c], fin[1, c]], axis=1)
    other_half = jnp.concatenate([dn[0], dn[1]], axis=1)
    dnorm = jnp.concatenate(
        [jnp.where(c == 0, own_half, other_half), jnp.where(c == 0, other_half, own_half)],
        axis=1,
    )
    scaled = gain * dnorm
    hg = (scaled - xhat * jnp.mean(scaled * xhat, axis=-1, keepdims=True)) / rms
    hg_ref[...] = hg.astype(BF16)

    next(xk)
    weight_part(Dk, acck, dwk_ref, 1)
    weight_part(Dk, acck, dwk_ref, 3)
    next(xk, None)
    weight_part(Dk, acck, dwk_ref, 2)
    for cp in sends.values():
        cp.wait_send()
    for j in range(2):
        @pl.when(2 * c + j != x)
        def _():
            pltpu.make_async_remote_copy(
                src_ref=G.at[2 * c + j], dst_ref=E.at[0], send_sem=esend.at[j],
                recv_sem=erecv.at[0], device_id=sibling, device_id_type=MESH,
            ).wait_send()
    for cp in handed:
        @pl.when(c == owner)
        def _():
            cp.wait_send()
    assert count[0] == NSEM, count[0]


def place(dq, dwk, dwv, hg, dg, dq_out, dwk_out, dwv_out, hg_out, dg_out, sem):
    copies = []
    for src, dst in ((dwk, dwk_out), (dwv, dwv_out), (dq, dq_out)):
        step = src.shape[0] // 4
        for p in range(4):
            rows = pl.ds(p * step, step)
            cp = pltpu.make_async_copy(src.at[rows], dst.at[rows], sem.at[len(copies)])
            cp.start()
            copies.append(cp)
    hg_out[...] = hg[...]
    dg_out[...] = dg[...]
    for cp in copies:
        cp.wait()


def local(enc_hidden, enc_gain, key_weight, value_weight, queries, cotangent, enc_len, dec_len):
    vmem = pl.BlockSpec(memory_space=pltpu.VMEM)
    hbm = pl.BlockSpec(memory_space=pl.ANY)
    smem = pl.BlockSpec(memory_space=pltpu.SMEM)
    v = pltpu.VMEM
    shapes = (
        jax.ShapeDtypeStruct((DEC, WID), BF16),
        jax.ShapeDtypeStruct((QC, WID), BF16),
        jax.ShapeDtypeStruct((QC, WID), BF16),
        jax.ShapeDtypeStruct((8, D), BF16),
        jax.ShapeDtypeStruct((1, D), F32),
    )
    outs = pl.pallas_call(
        kernel,
        out_shape=tuple(v(o.shape, o.dtype) for o in shapes),
        in_specs=[vmem, vmem, hbm, hbm, vmem, vmem, smem, smem],
        out_specs=(vmem,) * 5,
        scratch_shapes=[
            v((D, WID), BF16),
            v((D, WID), BF16),
            pltpu.SemaphoreType.DMA((2,)),
            v((8, D), F32),
            v((8, D // 2), F32),
            v((4, NY, NZ, 16, QC), BF16),
            v((3, NY, NZ, 16, QC), BF16),
            v((ROWS, WID), F32),
            v((ROWS, WID), BF16),
            v((ROWS, WID), BF16),
            v((2, ROWS, DEC), F32),
            v((DEC, WID), BF16),
            v((2, ROWS, DEC), BF16),
            v((4, ROWS, WID), BF16),
            v((4, ROWS, WID), BF16),
            v((2, NY, NZ, 16, QC), BF16),
            v((2, NY, NZ, 16, QC), BF16),
            v((2, NY, NZ, 16, QC), F32),
            [v((3, NZ, 16, QC), BF16), v((3, 16, QC), BF16)],
            [v((7, 16, QC), BF16), v((8, 2, 2, 16, QC), BF16)],
            [v((3, NZ, 16, QC), BF16), v((3, 16, QC), BF16)],
            [v((7, 16, QC), BF16), v((8, 2, 2, 16, QC), BF16)],
            v((2, 2, 8, QC), F32),
            v((2, 8, QC), F32),
            v((QC, WID), F32),
            v((QC, WID), F32),
            v((NZ, 8, 256), F32),
            v((NY, 8, 256), F32),
            v((NX, 8, 256), F32),
            v((2, 8, 256), F32),
            pltpu.SemaphoreType.DMA((NSEND,)),
            pltpu.SemaphoreType.DMA((NSEM,)),
            pltpu.SemaphoreType.DMA((5,)),
            pltpu.SemaphoreType.DMA((6,)),
        ],
        compiler_params=pltpu.CompilerParams(
            collective_id=0, has_side_effects=True, vmem_limit_bytes=52 * 1024 * 1024
        ),
        cost_estimate=pl.CostEstimate(
            flops=15_000_000_000, bytes_accessed=12_000_000, transcendentals=300_000
        ),
    )(
        enc_hidden[0], enc_gain, key_weight[0, 0], value_weight[0, 0],
        queries[0, 0], cotangent[0, 0], enc_len, dec_len,
    )
    dq, dwk, dwv, hg, dg = pl.pallas_call(
        place,
        out_shape=shapes,
        in_specs=[vmem] * 5,
        out_specs=(hbm, hbm, hbm, vmem, vmem),
        scratch_shapes=[pltpu.SemaphoreType.DMA((12,))],
    )(*[pltpu.with_memory_space_constraint(o, pltpu.VMEM) for o in outs])
    return dq[None, None], dwk[None], dwv[None], hg[None], dg[0]


def solution(mesh):
    placed = (
        P("replica", ("section", "tensor"), None),
        P("replica", None),
        P("replica", "section", None, "tensor"),
        P("replica", "section", None, "tensor"),
        P("replica", "section", None, "tensor"),
        P("replica", "section", None, "tensor"),
        P("replica"),
        P("replica"),
    )
    return jax.shard_map(
        local,
        mesh=mesh,
        in_specs=placed,
        out_specs=(
            P("replica", "section", None, "tensor"),
            P("section", "replica", "tensor"),
            P("section", "replica", "tensor"),
            P("replica", ("section", "tensor"), None),
            P(),
        ),
        check_vma=False,
    )
```

```python
import jax
import jax.numpy as jnp
from jax import lax
from jax.experimental import pallas as pl
from jax.experimental.pallas import tpu as pltpu
from jax.sharding import PartitionSpec as P

MESH = pl.DeviceIdType.MESH
F32 = jnp.float32
BF16 = jnp.bfloat16
D = 4096
ROWS = 512
DEC = 256
HD = 256
WID = 512
NX, NY, NZ = 4, 4, 8
QC = D // 4
HC = QC // 2
EC = QC // 4
NSEM = 173
NSEND = 48


def dot(a, b, ca=1, cb=0):
    return lax.dot_general(a, b, (((ca,), (cb,)), ((), ())), preferred_element_type=F32)


def kernel(
    hid_ref, gain_ref, kw_ref, vw_ref, q_ref, ct_ref, elen_ref, dlen_ref,
    dq_ref, dwk_ref, dwv_ref, hg_ref, dg_ref,
    wk, wv, wsem, n32, x32, G, E, acc, keys, vals, probs, grad, dsc, Dv, Dk,
    Ts, Tr, To, ly, lz, sy, sz, fin, dn, accv, acck,
    gz, gy, gx, gf, ssem, rsem, esend, erecv, zsem,
):
    x = lax.axis_index("replica")
    sec = lax.axis_index("section")
    zlo = lax.axis_index("tensor")
    c = lax.rem(sec, 2)
    y = lax.rem(lax.div(sec, 2), NY)
    z = lax.div(sec, 2 * NY) * 4 + zlo
    sib = 1 - c

    def dev(dx=0, dy=0, dz=0, core=None):
        xx = lax.rem(x + dx + NX, NX)
        yy = lax.rem(y + dy + NY, NY)
        zz = lax.rem(z + dz + NZ, NZ)
        cc = c if core is None else core
        return (xx, (lax.div(zz, 4) * NY + yy) * 2 + cc, lax.rem(zz, 4))

    def xo(d):
        return lax.rem(x + d + NX, NX)

    def yo(d):
        return lax.rem(y + d + NY, NY)

    def zo(d):
        return lax.rem(z + d + NZ, NZ)

    sibling = dev(core=sib)
    count = [0]
    sends = {}

    def put(src, dst, to):
        i = count[0]
        count[0] += 1
        s = i % NSEND
        if s in sends:
            sends[s].wait_send()
        cp = pltpu.make_async_remote_copy(
            src_ref=src, dst_ref=dst, send_sem=ssem.at[s], recv_sem=rsem.at[i],
            device_id=to, device_id_type=MESH,
        )
        cp.start()
        sends[s] = cp
        return i

    def got(i, region):
        pltpu.make_async_remote_copy(
            src_ref=region, dst_ref=region, send_sem=ssem.at[0], recv_sem=rsem.at[i],
            device_id=sibling, device_id_type=MESH,
        ).wait_recv()

    background = []

    def poll(n=1):
        for _ in range(n):
            for g in list(background):
                if next(g, "end") == "end":
                    background.remove(g)

    def drain():
        while background:
            poll()

    wcopies = [
        pltpu.make_async_copy(kw_ref, wk, wsem.at[0]),
        pltpu.make_async_copy(vw_ref, wv, wsem.at[1]),
    ]
    for w in wcopies:
        w.start()

    partners = [sibling]
    partners += [dev(dz=d) for d in range(1, NZ)]
    partners += [dev(dy=d) for d in range(1, NY)]
    partners += [dev(dx=d, core=e) for d in range(1, NX) for e in (c, sib)]
    barrier = pltpu.get_barrier_semaphore()
    for p in partners:
        pl.semaphore_signal(barrier, inc=1, device_id=p, device_id_type=MESH)

    hid = hid_ref[...].astype(F32)
    gain = gain_ref[...].astype(F32)
    rms = jnp.sqrt(jnp.mean(hid * hid, axis=-1, keepdims=True) + 1e-06)
    xhat = hid / rms
    n32[...] = (xhat * gain).astype(BF16).astype(F32)
    pl.semaphore_wait(barrier, len(partners))

    hc = D // 2
    i = put(n32.at[:, pl.ds(pl.multiple_of(sib * hc, hc), hc)], x32, sibling)
    mine = jnp.where(c == 0, n32[:, :hc], n32[:, hc:])
    got(i, x32)
    other = x32[...]
    chip = jnp.concatenate(
        [jnp.where(c == 0, mine, other), jnp.where(c == 0, other, mine)], axis=0
    ).astype(BF16)
    for j in range(2):
        G[2 * c + j, y, z] = chip[:, j * QC:(j + 1) * QC]

    arrivals = []

    def forward(region):
        i = put(region(c), region(c), sibling)
        arrivals.append((i, region(sib)))

    def cols_to(j, half):
        q = 2 * c + j
        slot = jnp.maximum(lax.rem(x - q + NX, NX) - 1, 0)
        return pltpu.make_async_remote_copy(
            src_ref=G.at[q, y, z, :, pl.ds(half * HC, HC)], dst_ref=E.at[half, slot, y, z],
            send_sem=esend.at[2 * j + half], recv_sem=erecv.at[slot],
            device_id=dev(dx=q - x, core=half), device_id_type=MESH,
        )

    def each_cols(act):
        for j in range(2):
            @pl.when(2 * c + j != x)
            def _():
                for half in range(2):
                    act(cols_to(j, half))

    ydist = (1, 3, 2)

    def plane_gather(slab_a, slab_b, chunk_b, over_a, over_b):
        def along_y(slab, zz):
            return [put(slab(y, zz), slab(y, zz), dev(dy=d)) for d in ydist]

        b_y = along_y(slab_b, z)
        a_z = {d: put(slab_a(y, z), slab_a(y, z), dev(dz=d)) for d in (1, 7, 2, 6, 3, 5, 4)}
        a_y = {0: along_y(slab_a, z)}

        def from_z(*dist):
            for d in dist:
                got(a_z[d], slab_a(y, zo(-d)))
                a_y[d] = along_y(slab_a, zo(-d))

        def from_y(*dist):
            for e in dist:
                for d, i in zip(ydist, a_y[e]):
                    got(i, slab_a(yo(-d), zo(-e)))

        yield
        from_z(1, 7)
        for d, i in zip(ydist, b_y):
            got(i, slab_b(yo(-d), z))
        right = {h: put(chunk_b(z, h), chunk_b(z, h), dev(dz=1)) for h in (0, 1)}
        left = {h: put(chunk_b(z, h), chunk_b(z, h), dev(dz=-1)) for h in (1, 0)}
        forward(lambda cc: over_b(cc, z))

        def hop(k):
            for h in (0, 1):
                zr, zl = zo(-k), zo(k)
                if k < 4 or h == 0:
                    got(right[h], chunk_b(zr, h))
                    if k < 3 or (k == 3 and h == 0):
                        right[h] = put(chunk_b(zr, h), chunk_b(zr, h), dev(dz=1))
                g = 1 - h
                if k < 4 or g == 1:
                    got(left[g], chunk_b(zl, g))
                    if k < 3 or (k == 3 and g == 1):
                        left[g] = put(chunk_b(zl, g), chunk_b(zl, g), dev(dz=-1))
            forward(lambda cc: over_b(cc, zo(-k)))
            if k < 4:
                forward(lambda cc: over_b(cc, zo(k)))

        from_z(2, 6, 3, 5)
        yield
        hop(1)
        from_z(4)
        forward(lambda cc: over_a(cc, y))
        yield
        from_y(0, 1, 7)
        hop(2)
        yield
        from_y(2, 6)
        hop(3)
        yield
        from_y(3, 5, 4)
        for d in ydist:
            yy = yo(-d)
            forward(lambda cc: over_a(cc, yy))
        hop(4)

    ga = plane_gather(
        lambda yy, zz: G.at[2 * c, yy, zz],
        lambda yy, zz: G.at[2 * c + 1, yy, zz],
        lambda zz, h: G.at[2 * c + 1, pl.ds(2 * h, 2), zz],
        lambda cc, yy: G.at[2 * cc, yy],
        lambda cc, zz: G.at[2 * cc + 1, :, zz],
    )
    next(ga)
    each_cols(lambda cp: cp.start())
    for _ in ga:
        pass
    whole = list(arrivals)
    arrivals.clear()

    lo, hi = pl.ds(0, EC), pl.ds(EC, EC)
    every = slice(None)
    ea = plane_gather(
        lambda yy, zz: E.at[c, :, yy, zz, :, lo],
        lambda yy, zz: E.at[c, :, yy, zz, :, hi],
        lambda zz, h: E.at[c, :, pl.ds(2 * h, 2), zz, :, hi],
        lambda cc, yy: E.at[cc, :, yy, :, :, lo],
        lambda cc, zz: E.at[cc, :, :, zz, :, hi],
    )
    for k in range(3):
        slab = E.at[c, k, y, z]
        pltpu.make_async_remote_copy(
            src_ref=slab, dst_ref=slab, send_sem=esend.at[0], recv_sem=erecv.at[k],
            device_id=sibling, device_id_type=MESH,
        ).wait_recv()
    next(ea)

    def project(w, out, first):
        for j in range(4):
            if first and j == 2:
                for i, region in whole:
                    got(i, region)
            q = lax.rem(2 * c + j, 4)
            part = dot(G[q].reshape(ROWS, QC), w[pl.ds(pl.multiple_of(q * QC, QC), QC), :])
            if j == 0:
                acc[...] = part
            elif j < 3:
                acc[...] += part
            else:
                out[...] = (acc[...] + part).astype(BF16)

    scale = HD ** (-0.5)
    row = lax.broadcasted_iota(jnp.int32, (ROWS, 1), 0)
    inner = row & 7
    row_c = (row >> 3) & 1
    row_z = (row >> 4) & 7
    row_y = row >> 7
    pos = ((((row_z >> 2) * NY + row_y) * 2 + row_c) * 4 + (row_z & 3)) * 8 + inner
    keep = pos < elen_ref[0]
    live = lax.broadcasted_iota(jnp.int32, (DEC, 1), 0) < dlen_ref[0]
    grad[...] = jnp.where(live, ct_ref[...], jnp.zeros((DEC, WID), BF16))
    wcopies[0].wait()
    project(wk, keys, True)
    for h in range(2):
        cols = slice(h * HD, (h + 1) * HD)
        s = dot(keys[:, cols], q_ref[:, cols], 1, 1) * scale
        s = jnp.where(keep, s, -1e30)
        top = jnp.max(s, axis=0, keepdims=True)
        e = jnp.where(keep, jnp.exp(s - top), 0.0)
        p = e / jnp.sum(e, axis=0, keepdims=True)
        probs[h] = p
        Dv[0, :, cols] = dot(p.astype(BF16), grad[:, cols]).astype(BF16)

    def along_x(buf):
        def at(slot, h):
            return buf.at[slot, pl.ds(h * (ROWS // 2), ROWS // 2)]

        a0 = put(at(0, 0), at(3, 0), dev(dx=1))
        b1 = put(at(0, 1), at(1, 1), dev(dx=-1))
        a1 = put(at(0, 1), at(3, 1), dev(dx=1))
        b0 = put(at(0, 0), at(1, 0), dev(dx=-1))
        yield
        got(a0, at(3, 0))
        f0 = put(at(3, 0), at(2, 0), dev(dx=1))
        got(b1, at(1, 1))
        f1 = put(at(1, 1), at(2, 1), dev(dx=-1))
        yield
        got(a1, at(3, 1))
        got(b0, at(1, 0))
        yield
        got(f0, at(2, 0))
        got(f1, at(2, 1))

    xv = along_x(Dv)
    next(xv)
    wcopies[1].wait()
    project(wv, vals, False)
    next(ea)
    for h in range(2):
        cols = slice(h * HD, (h + 1) * HD)
        dp = dot(vals[:, cols], grad[:, cols], 1, 1)
        p = probs[h]
        ds = (p * (dp - jnp.sum(p * dp, axis=0, keepdims=True))).astype(BF16)
        dsc[h] = ds
        Dk[0, :, cols] = (dot(ds, q_ref[:, cols]) * scale).astype(BF16)
    xk = along_x(Dk)
    next(xk)

    def slab_to(zz):
        to = (x, (zz // 4 * NY + y) * 2 + c, zz % 4)
        return pltpu.make_async_remote_copy(
            src_ref=sz[0].at[zz], dst_ref=lz[0].at[z], send_sem=zsem.at[zz],
            recv_sem=zsem.at[NZ], device_id=to, device_id_type=MESH,
        )

    def sum_y_first():
        order = (2, 1, 3)
        idx = {}
        for h in range(2):
            zs = pl.ds(4 * h, 4)
            for d in order:
                sy[0][d - 1, zs] = To[0, yo(d), zs].astype(BF16)
                idx[h, d] = put(sy[0].at[d - 1, zs], ly[0].at[d - 1, zs], dev(dy=d))
        lz[0][z] = jnp.zeros((16, QC), BF16)
        yield
        for h in range(2):
            yield
            zs = pl.ds(4 * h, 4)
            for d in order:
                got(idx[h, d], ly[0].at[d - 1, zs])
            v = To[0, y, zs]
            for d in range(3):
                v = v + ly[0][d, zs].astype(F32)
            To[0, y, zs] = v
            sz[0][zs] = v.astype(BF16)
            for zz in range(4 * h, 4 * h + 4):
                @pl.when(zz != z)
                def _():
                    slab_to(zz).start()
        yield
        yield
        got_all = lz[0].at[pl.ds(0, 7)]
        pltpu.make_async_remote_copy(
            src_ref=got_all, dst_ref=got_all, send_sem=zsem.at[0], recv_sem=zsem.at[NZ],
            device_id=sibling, device_id_type=MESH,
        ).wait_recv()
        v = To[0, y, z]
        for d in range(NZ):
            v = v + lz[0][d].astype(F32)
        fin[0] = v.reshape(2, 8, QC)

    def sum_z_first():
        stage, land = sz[1], lz[1]

        def own(zz, h):
            return To[1, 2 * h:2 * h + 2, zz]

        def send(slot, h, value, to):
            stage[slot, h] = value.astype(BF16)
            return put(stage.at[slot, h], land.at[slot, h], to)

        a, b = [None, None], [None, None]
        a[0] = send(0, 0, own(zo(4), 0), dev(dz=1))
        b[1] = send(4, 1, own(zo(4), 1), dev(dz=-1))
        a[1] = send(1, 1, own(zo(3), 1), dev(dz=1))
        b[0] = send(5, 0, own(zo(-3), 0), dev(dz=-1))
        for s, k in ((1, 3), (2, 2), (3, 1)):
            yield
            for h in ((0, 1) if s > 1 else (0,)):
                got(a[h], land.at[s - 1, h])
                a[h] = send(s, h, own(zo(k), h) + land[s - 1, h].astype(F32), dev(dz=1))
                g = 1 - h
                got(b[g], land.at[3 + s, g])
                b[g] = send(4 + s, g, own(zo(-k), g) + land[3 + s, g].astype(F32), dev(dz=-1))
        yield
        for h in range(2):
            got(a[h], land.at[3, h])
            got(b[h], land.at[7, h])
            To[1, 2 * h:2 * h + 2, z] = (
                own(z, h) + land[3, h].astype(F32) + land[7, h].astype(F32)
            )
        order = (2, 1, 3)
        idx = []
        for d in order:
            sy[1][d - 1] = To[1, yo(d), z].astype(BF16)
            idx.append(put(sy[1].at[d - 1], ly[1].at[d - 1], dev(dy=d)))
        yield
        for d, i in zip(order, idx):
            got(i, ly[1].at[d - 1])
        v = To[1, y, z]
        for d in range(3):
            v = v + ly[1][d].astype(F32)
        fin[1] = v.reshape(2, 8, QC)

    t_in = {}
    sums = {1: sum_z_first(), 0: sum_y_first()}
    for core, j in ((sib, 1), (sib, 0), (c, 1), (c, 0)):
        w = pl.ds(pl.multiple_of((2 * core + j) * QC, QC), QC)
        t = dot(Dk[0], wk[w, :], 1, 1) + dot(Dv[0], wv[w, :], 1, 1)
        if core is sib:
            Ts[j] = t.astype(BF16).reshape(NY, NZ, 16, QC)
            t_in[j] = put(Ts.at[j], Tr.at[j], sibling)
        else:
            got(t_in[j], Tr.at[j])
            To[j] = t.reshape(NY, NZ, 16, QC) + Tr[j].astype(F32)
            next(sums[j])
        if j == 0:
            next(ea)
    next(xv)

    gsel = jnp.where(c == 0, gain[:, :hc], gain[:, hc:])
    for j in range(2):
        prod = To[j].reshape(ROWS, QC) * G[2 * c + j].reshape(ROWS, QC).astype(F32)
        terms = jnp.sum(prod, axis=0, keepdims=True) / gsel[:, j * QC:(j + 1) * QC]
        for r in range(4):
            gz[z, 4 * j + r:4 * j + r + 1, :] = terms[:, r * 256:(r + 1) * 256]

    def sum_gain():
        idx = [(put(gz.at[z], gz.at[z], dev(dz=d)), zo(-d)) for d in range(1, NZ)]
        yield
        for i, s in idx:
            got(i, gz.at[s])
        gy[y] = jnp.sum(gz[...], axis=0)
        idx = [(put(gy.at[y], gy.at[y], dev(dy=d)), yo(-d)) for d in range(1, NY)]
        yield
        for i, s in idx:
            got(i, gy.at[s])
        gx[x] = jnp.sum(gy[...], axis=0)
        idx = [(put(gx.at[x], gx.at[x], dev(dx=d)), xo(-d)) for d in range(1, NX)]
        yield
        for i, s in idx:
            got(i, gx.at[s])
        gf[c] = jnp.sum(gx[...], axis=0) / NX
        i = put(gf.at[c], gf.at[c], sibling)
        yield
        got(i, gf.at[sib])
        for h in range(2):
            for r in range(8):
                lo = h * hc + r * 256
                dg_ref[0:1, lo:lo + 256] = gf[h, r:r + 1, :]

    def weight_part(buf, total, out, k):
        for q in range(4):
            r = slice(q * EC, (q + 1) * EC)
            half = slice(q % 2 * EC, (q % 2 + 1) * EC)
            if k == 0:
                cols = G[x, :, :, :, r]
            else:
                cols = E[q // 2, k - 1, :, :, :, half]
            part = dot(cols.reshape(ROWS, EC), buf[k], 0, 0)
            if k == 0:
                total[r, :] = part
            elif k == 2:
                out[r, :] = ((total[r, :] + part) / NX).astype(BF16)
            else:
                total[r, :] += part

    background += [sums[1], sums[0], sum_gain()]
    poll()
    for h in range(2):
        cols = slice(h * HD, (h + 1) * HD)
        dq_ref[:, cols] = (dot(dsc[h], keys[:, cols], 0, 0) * scale).astype(BF16)
    weight_part(Dv, accv, dwv_ref, 0)
    poll()
    next(ea)
    weight_part(Dk, acck, dwk_ref, 0)
    poll()
    next(ea, None)
    next(xv)
    poll()
    for i, region in arrivals:
        got(i, region)
    weight_part(Dv, accv, dwv_ref, 1)
    weight_part(Dv, accv, dwv_ref, 3)
    next(xk)
    poll()
    next(xv, None)
    weight_part(Dv, accv, dwv_ref, 2)
    drain()

    i = put(fin.at[:, sib], dn, sibling)
    got(i, dn)
    own_half = jnp.concatenate([fin[0, c], fin[1, c]], axis=1)
    other_half = jnp.concatenate([dn[0], dn[1]], axis=1)
    dnorm = jnp.concatenate(
        [jnp.where(c == 0, own_half, other_half), jnp.where(c == 0, other_half, own_half)],
        axis=1,
    )
    scaled = gain * dnorm
    hg = (scaled - xhat * jnp.mean(scaled * xhat, axis=-1, keepdims=True)) / rms
    hg_ref[...] = hg.astype(BF16)

    next(xk)
    weight_part(Dk, acck, dwk_ref, 1)
    weight_part(Dk, acck, dwk_ref, 3)
    next(xk, None)
    weight_part(Dk, acck, dwk_ref, 2)
    for cp in sends.values():
        cp.wait_send()
    each_cols(lambda cp: cp.wait_send())
    for d in range(NZ):
        @pl.when(d != z)
        def _():
            slab_to(d).wait_send()
    assert count[0] == NSEM, count[0]


def place(dq, dwk, dwv, hg, dg, dq_out, dwk_out, dwv_out, hg_out, dg_out, sem):
    copies = []
    for src, dst in ((dwk, dwk_out), (dwv, dwv_out), (dq, dq_out)):
        step = src.shape[0] // 4
        for p in range(4):
            rows = pl.ds(p * step, step)
            cp = pltpu.make_async_copy(src.at[rows], dst.at[rows], sem.at[len(copies)])
            cp.start()
            copies.append(cp)
    hg_out[...] = hg[...]
    dg_out[...] = dg[...]
    for cp in copies:
        cp.wait()


def local(enc_hidden, enc_gain, key_weight, value_weight, queries, cotangent, enc_len, dec_len):
    vmem = pl.BlockSpec(memory_space=pltpu.VMEM)
    hbm = pl.BlockSpec(memory_space=pl.ANY)
    smem = pl.BlockSpec(memory_space=pltpu.SMEM)
    v = pltpu.VMEM
    shapes = (
        jax.ShapeDtypeStruct((DEC, WID), BF16),
        jax.ShapeDtypeStruct((QC, WID), BF16),
        jax.ShapeDtypeStruct((QC, WID), BF16),
        jax.ShapeDtypeStruct((8, D), BF16),
        jax.ShapeDtypeStruct((1, D), F32),
    )
    outs = pl.pallas_call(
        kernel,
        out_shape=tuple(v(o.shape, o.dtype) for o in shapes),
        in_specs=[vmem, vmem, hbm, hbm, vmem, vmem, smem, smem],
        out_specs=(vmem,) * 5,
        scratch_shapes=[
            v((D, WID), BF16),
            v((D, WID), BF16),
            pltpu.SemaphoreType.DMA((2,)),
            v((8, D), F32),
            v((8, D // 2), F32),
            v((4, NY, NZ, 16, QC), BF16),
            v((2, 3, NY, NZ, 16, HC), BF16),
            v((ROWS, WID), F32),
            v((ROWS, WID), BF16),
            v((ROWS, WID), BF16),
            v((2, ROWS, DEC), F32),
            v((DEC, WID), BF16),
            v((2, ROWS, DEC), BF16),
            v((4, ROWS, WID), BF16),
            v((4, ROWS, WID), BF16),
            v((2, NY, NZ, 16, QC), BF16),
            v((2, NY, NZ, 16, QC), BF16),
            v((2, NY, NZ, 16, QC), F32),
            [v((3, NZ, 16, QC), BF16), v((3, 16, QC), BF16)],
            [v((NZ, 16, QC), BF16), v((8, 2, 2, 16, QC), BF16)],
            [v((3, NZ, 16, QC), BF16), v((3, 16, QC), BF16)],
            [v((NZ, 16, QC), BF16), v((8, 2, 2, 16, QC), BF16)],
            v((2, 2, 8, QC), F32),
            v((2, 8, QC), F32),
            v((QC, WID), F32),
            v((QC, WID), F32),
            v((NZ, 8, 256), F32),
            v((NY, 8, 256), F32),
            v((NX, 8, 256), F32),
            v((2, 8, 256), F32),
            pltpu.SemaphoreType.DMA((NSEND,)),
            pltpu.SemaphoreType.DMA((NSEM,)),
            pltpu.SemaphoreType.DMA((4,)),
            pltpu.SemaphoreType.DMA((3,)),
            pltpu.SemaphoreType.DMA((NZ + 1,)),
        ],
        compiler_params=pltpu.CompilerParams(
            collective_id=0, has_side_effects=True, vmem_limit_bytes=52 * 1024 * 1024
        ),
        cost_estimate=pl.CostEstimate(
            flops=15_000_000_000, bytes_accessed=12_000_000, transcendentals=300_000
        ),
    )(
        enc_hidden[0], enc_gain, key_weight[0, 0], value_weight[0, 0],
        queries[0, 0], cotangent[0, 0], enc_len, dec_len,
    )
    dq, dwk, dwv, hg, dg = pl.pallas_call(
        place,
        out_shape=shapes,
        in_specs=[vmem] * 5,
        out_specs=(hbm, hbm, hbm, vmem, vmem),
        scratch_shapes=[pltpu.SemaphoreType.DMA((12,))],
    )(*[pltpu.with_memory_space_constraint(o, pltpu.VMEM) for o in outs])
    return dq[None, None], dwk[None], dwv[None], hg[None], dg[0]


def solution(mesh):
    placed = (
        P("replica", ("section", "tensor"), None),
        P("replica", None),
        P("replica", "section", None, "tensor"),
        P("replica", "section", None, "tensor"),
        P("replica", "section", None, "tensor"),
        P("replica", "section", None, "tensor"),
        P("replica"),
        P("replica"),
    )
    return jax.shard_map(
        local,
        mesh=mesh,
        in_specs=placed,
        out_specs=(
            P("replica", "section", None, "tensor"),
            P("section", "replica", "tensor"),
            P("section", "replica", "tensor"),
            P("replica", ("section", "tensor"), None),
            P(),
        ),
        check_vma=False,
    )
```

```python
import jax
import jax.numpy as jnp
from jax import lax
from jax.experimental import pallas as pl
from jax.experimental.pallas import tpu as pltpu
from jax.sharding import PartitionSpec as P

MESH = pl.DeviceIdType.MESH
F32 = jnp.float32
BF16 = jnp.bfloat16
D = 4096
ROWS = 512
DEC = 256
HD = 256
WID = 512
NX, NY, NZ = 4, 4, 8
QC = D // 4
HC = QC // 2
EC = QC // 4
NSEM = 89
NSEND = 112


def dot(a, b, ca=1, cb=0):
    return lax.dot_general(a, b, (((ca,), (cb,)), ((), ())), preferred_element_type=F32)


def kernel(
    hid_ref, gain_ref, kw_ref, vw_ref, q_ref, ct_ref, elen_hbm, dlen_hbm,
    dq_ref, dwk_ref, dwv_ref, hg_ref, dg_ref,
    wk, wv, wsem, elen_ref, dlen_ref, n32, x32, G, E, acc, keys, vals, probs, grad, dsc, Dv, Dk,
    Ts, Tr, To, ly, lz, sy, sz, fin, dn, accv, acck,
    gz, gy, gx, gf, ssem, rsem, esend, erecv, zsem,
):
    x = lax.axis_index("replica")
    sec = lax.axis_index("section")
    zlo = lax.axis_index("tensor")
    c = lax.rem(sec, 2)
    y = lax.rem(lax.div(sec, 2), NY)
    z = lax.div(sec, 2 * NY) * 4 + zlo
    sib = 1 - c

    def dev(dx=0, dy=0, dz=0, core=None):
        xx = lax.rem(x + dx + NX, NX)
        yy = lax.rem(y + dy + NY, NY)
        zz = lax.rem(z + dz + NZ, NZ)
        cc = c if core is None else core
        return (xx, (lax.div(zz, 4) * NY + yy) * 2 + cc, lax.rem(zz, 4))

    def xo(d):
        return lax.rem(x + d + NX, NX)

    def yo(d):
        return lax.rem(y + d + NY, NY)

    def zo(d):
        return lax.rem(z + d + NZ, NZ)

    sibling = dev(core=sib)
    count = [0]
    order = [0]
    sends = {}

    def group():
        count[0] += 1
        return count[0] - 1

    def put(src, dst, to, i=None):
        i = group() if i is None else i
        s = order[0] % NSEND
        order[0] += 1
        if s in sends:
            sends[s].wait_send()
        cp = pltpu.make_async_remote_copy(
            src_ref=src, dst_ref=dst, send_sem=ssem.at[s], recv_sem=rsem.at[i],
            device_id=to, device_id_type=MESH,
        )
        cp.start()
        sends[s] = cp
        return i

    def got(i, region):
        pltpu.make_async_remote_copy(
            src_ref=region, dst_ref=region, send_sem=ssem.at[0], recv_sem=rsem.at[i],
            device_id=sibling, device_id_type=MESH,
        ).wait_recv()

    background = []

    def poll(n=1):
        for _ in range(n):
            for g in list(background):
                if next(g, "end") == "end":
                    background.remove(g)

    def drain():
        while background:
            poll()

    wcopies = [
        pltpu.make_async_copy(kw_ref, wk, wsem.at[0]),
        pltpu.make_async_copy(vw_ref, wv, wsem.at[1]),
        pltpu.make_async_copy(elen_hbm, elen_ref, wsem.at[2]),
        pltpu.make_async_copy(dlen_hbm, dlen_ref, wsem.at[3]),
    ]
    for w in wcopies:
        w.start()

    partners = [sibling]
    partners += [dev(dz=d) for d in range(1, NZ)]
    partners += [dev(dy=d) for d in range(1, NY)]
    partners += [dev(dx=d, core=e) for d in range(1, NX) for e in (c, sib)]
    barrier = pltpu.get_barrier_semaphore()
    for p in partners:
        pl.semaphore_signal(barrier, inc=1, device_id=p, device_id_type=MESH)

    hid = hid_ref[...].astype(F32)
    gain = gain_ref[...].astype(F32)
    rms = jnp.sqrt(jnp.mean(hid * hid, axis=-1, keepdims=True) + 1e-06)
    xhat = hid / rms
    n32[...] = (xhat * gain).astype(BF16).astype(F32)
    pl.semaphore_wait(barrier, len(partners))

    hc = D // 2
    i = put(n32.at[:, pl.ds(pl.multiple_of(sib * hc, hc), hc)], x32, sibling)
    mine = jnp.where(c == 0, n32[:, :hc], n32[:, hc:])
    got(i, x32)
    other = x32[...]
    chip = jnp.concatenate(
        [jnp.where(c == 0, mine, other), jnp.where(c == 0, other, mine)], axis=0
    ).astype(BF16)
    for j in range(2):
        G[2 * c + j, y, z] = chip[:, j * QC:(j + 1) * QC]

    def cols_to(j, half):
        q = 2 * c + j
        slot = jnp.maximum(lax.rem(x - q + NX, NX) - 1, 0)
        return pltpu.make_async_remote_copy(
            src_ref=G.at[q, y, z, :, pl.ds(half * HC, HC)], dst_ref=E.at[half, slot, y, z],
            send_sem=esend.at[2 * j + half], recv_sem=erecv.at[slot],
            device_id=dev(dx=q - x, core=half), device_id_type=MESH,
        )

    def each_cols(act):
        for j in range(2):
            @pl.when(2 * c + j != x)
            def _():
                for half in range(2):
                    act(cols_to(j, half))

    ydist = (1, 3, 2)

    def plane_gather(slab_a, half_a, slab_b, chunk_b, over_a, over_b, some_a, some_b, over):
        def forward(region):
            put(region(c), region(c), sibling, over)

        def along_y(slab, zz, i):
            for d in ydist:
                put(slab(y, zz), slab(y, zz), dev(dy=d), i)

        b_y = group()
        along_y(slab_b, z, b_y)
        a_z = {d: put(slab_a(y, z), slab_a(y, z), dev(dz=d)) for d in (1, 7, 2, 6, 3, 5, 4)}
        a_y = {e: group() for e in (0, 2, 3)}
        group_of = {0: 0, 1: 0, 7: 0, 2: 2, 6: 2, 3: 3, 5: 3, 4: 3}
        along_y(slab_a, z, a_y[0])

        def from_z(*dist):
            for d in dist:
                zz = zo(-d)
                got(a_z[d], slab_a(y, zz))
                along_y(slab_a, zz, a_y[group_of[d]])

        def from_y(e, n):
            got(a_y[e], some_a(n))

        yield
        from_z(1, 7)
        got(b_y, some_b())
        right = {h: put(chunk_b(z, h), chunk_b(z, h), dev(dz=1)) for h in (0, 1)}
        left = {h: put(chunk_b(z, h), chunk_b(z, h), dev(dz=-1)) for h in (1, 0)}
        forward(lambda cc: over_b(cc, z))

        def hop(k):
            for h in (0, 1):
                zr, zl = zo(-k), zo(k)
                if k < 4 or h == 0:
                    got(right[h], chunk_b(zr, h))
                    if k < 3 or (k == 3 and h == 0):
                        right[h] = put(chunk_b(zr, h), chunk_b(zr, h), dev(dz=1))
                g = 1 - h
                if k < 4 or g == 1:
                    got(left[g], chunk_b(zl, g))
                    if k < 3 or (k == 3 and g == 1):
                        left[g] = put(chunk_b(zl, g), chunk_b(zl, g), dev(dz=-1))
            forward(lambda cc: over_b(cc, zo(-k)))
            if k < 4:
                forward(lambda cc: over_b(cc, zo(k)))

        from_z(2, 6, 3, 5)
        yield
        hop(1)
        from_z(4)
        forward(lambda cc: over_a(cc, y))
        yield
        from_y(0, 3)
        hop(2)
        yield
        from_y(2, 2)
        hop(3)
        yield
        from_y(3, 3)
        for d in ydist:
            yy = yo(-d)
            forward(lambda cc: over_a(cc, yy))
        hop(4)

    g_over, e_over = group(), group()
    ga = plane_gather(
        lambda yy, zz: G.at[2 * c, yy, zz],
        lambda yy, zz, h: G.at[2 * c, yy, zz, :, pl.ds(h * HC, HC)],
        lambda yy, zz: G.at[2 * c + 1, yy, zz],
        lambda zz, h: G.at[2 * c + 1, pl.ds(2 * h, 2), zz],
        lambda cc, yy: G.at[2 * cc, yy],
        lambda cc, zz: G.at[2 * cc + 1, :, zz],
        lambda n: G.at[2 * c, pl.ds(0, 3), pl.ds(0, n)],
        lambda: G.at[2 * c + 1, pl.ds(0, 3), z],
        g_over,
    )
    next(ga)
    each_cols(lambda cp: cp.start())
    for _ in ga:
        pass

    lo, hi = pl.ds(0, EC), pl.ds(EC, EC)
    every = slice(None)
    ea = plane_gather(
        lambda yy, zz: E.at[c, :, yy, zz, :, lo],
        lambda yy, zz, h: E.at[c, :, yy, zz, :, pl.ds(h * (EC // 2), EC // 2)],
        lambda yy, zz: E.at[c, :, yy, zz, :, hi],
        lambda zz, h: E.at[c, :, pl.ds(2 * h, 2), zz, :, hi],
        lambda cc, yy: E.at[cc, :, yy, :, :, lo],
        lambda cc, zz: E.at[cc, :, :, zz, :, hi],
        lambda n: E.at[c, :, pl.ds(0, 3), pl.ds(0, n), :, lo],
        lambda: E.at[c, :, pl.ds(0, 3), z, :, hi],
        e_over,
    )
    for k in range(3):
        slab = E.at[c, k, y, z]
        pltpu.make_async_remote_copy(
            src_ref=slab, dst_ref=slab, send_sem=esend.at[0], recv_sem=erecv.at[k],
            device_id=sibling, device_id_type=MESH,
        ).wait_recv()
    next(ea)

    def project(w, out, first):
        for j in range(4):
            if first and j == 2:
                got(g_over, G.at[pl.ds(2 * sib, 2)])
            q = lax.rem(2 * c + j, 4)
            part = dot(G[q].reshape(ROWS, QC), w[pl.ds(pl.multiple_of(q * QC, QC), QC), :])
            if j == 0:
                acc[...] = part
            elif j < 3:
                acc[...] += part
            else:
                out[...] = (acc[...] + part).astype(BF16)

    scale = HD ** (-0.5)
    row = lax.broadcasted_iota(jnp.int32, (ROWS, 1), 0)
    inner = row & 7
    row_c = (row >> 3) & 1
    row_z = (row >> 4) & 7
    row_y = row >> 7
    pos = ((((row_z >> 2) * NY + row_y) * 2 + row_c) * 4 + (row_z & 3)) * 8 + inner
    wcopies[2].wait()
    wcopies[3].wait()
    keep = pos < elen_ref[0]
    live = lax.broadcasted_iota(jnp.int32, (DEC, 1), 0) < dlen_ref[0]
    grad[...] = jnp.where(live, ct_ref[...], jnp.zeros((DEC, WID), BF16))
    wcopies[0].wait()
    project(wk, keys, True)
    for h in range(2):
        cols = slice(h * HD, (h + 1) * HD)
        s = dot(keys[:, cols], q_ref[:, cols], 1, 1) * scale
        s = jnp.where(keep, s, -1e30)
        top = jnp.max(s, axis=0, keepdims=True)
        e = jnp.where(keep, jnp.exp(s - top), 0.0)
        p = e / jnp.sum(e, axis=0, keepdims=True)
        probs[h] = p
        Dv[0, :, cols] = dot(p.astype(BF16), grad[:, cols]).astype(BF16)

    def along_x(buf):
        def at(slot, h):
            return buf.at[slot, pl.ds(h * (ROWS // 2), ROWS // 2)]

        a0 = put(at(0, 0), at(3, 0), dev(dx=1))
        b1 = put(at(0, 1), at(1, 1), dev(dx=-1))
        a1 = put(at(0, 1), at(3, 1), dev(dx=1))
        b0 = put(at(0, 0), at(1, 0), dev(dx=-1))
        yield
        got(a0, at(3, 0))
        f0 = put(at(3, 0), at(2, 0), dev(dx=1))
        got(b1, at(1, 1))
        f1 = put(at(1, 1), at(2, 1), dev(dx=-1))
        yield
        got(a1, at(3, 1))
        got(b0, at(1, 0))
        yield
        got(f0, at(2, 0))
        got(f1, at(2, 1))

    xv = along_x(Dv)
    next(xv)
    wcopies[1].wait()
    project(wv, vals, False)
    next(ea)
    for h in range(2):
        cols = slice(h * HD, (h + 1) * HD)
        dp = dot(vals[:, cols], grad[:, cols], 1, 1)
        p = probs[h]
        ds = (p * (dp - jnp.sum(p * dp, axis=0, keepdims=True))).astype(BF16)
        dsc[h] = ds
        Dk[0, :, cols] = (dot(ds, q_ref[:, cols]) * scale).astype(BF16)
    xk = along_x(Dk)
    next(xk)

    def slab_to(zz):
        to = (x, (zz // 4 * NY + y) * 2 + c, zz % 4)
        return pltpu.make_async_remote_copy(
            src_ref=sz[0].at[zz], dst_ref=lz[0].at[z], send_sem=zsem.at[zz],
            recv_sem=zsem.at[NZ], device_id=to, device_id_type=MESH,
        )

    def sum_y_first():
        order = (2, 1, 3)
        idx = [group(), group()]
        for h in range(2):
            zs = pl.ds(4 * h, 4)
            for d in order:
                sy[0][d - 1, zs] = To[0, yo(d), zs].astype(BF16)
                put(sy[0].at[d - 1, zs], ly[0].at[d - 1, zs], dev(dy=d), idx[h])
        lz[0][z] = jnp.zeros((16, QC), BF16)
        yield
        for h in range(2):
            yield
            zs = pl.ds(4 * h, 4)
            got(idx[h], ly[0].at[:, zs])
            v = To[0, y, zs]
            for d in range(3):
                v = v + ly[0][d, zs].astype(F32)
            To[0, y, zs] = v
            sz[0][zs] = v.astype(BF16)
            for zz in range(4 * h, 4 * h + 4):
                @pl.when(zz != z)
                def _():
                    slab_to(zz).start()
        yield
        yield
        got_all = lz[0].at[pl.ds(0, 7)]
        pltpu.make_async_remote_copy(
            src_ref=got_all, dst_ref=got_all, send_sem=zsem.at[0], recv_sem=zsem.at[NZ],
            device_id=sibling, device_id_type=MESH,
        ).wait_recv()
        v = To[0, y, z]
        for d in range(NZ):
            v = v + lz[0][d].astype(F32)
        fin[0] = v.reshape(2, 8, QC)

    def sum_z_first():
        stage, land = sz[1], lz[1]

        def own(zz, h):
            return To[1, 2 * h:2 * h + 2, zz]

        def send(slot, h, value, to):
            stage[slot, h] = value.astype(BF16)
            return put(stage.at[slot, h], land.at[slot, h], to)

        a, b = [None, None], [None, None]
        a[0] = send(0, 0, own(zo(4), 0), dev(dz=1))
        b[1] = send(4, 1, own(zo(4), 1), dev(dz=-1))
        a[1] = send(1, 1, own(zo(3), 1), dev(dz=1))
        b[0] = send(5, 0, own(zo(-3), 0), dev(dz=-1))
        for s, k in ((1, 3), (2, 2), (3, 1)):
            yield
            for h in ((0, 1) if s > 1 else (0,)):
                got(a[h], land.at[s - 1, h])
                a[h] = send(s, h, own(zo(k), h) + land[s - 1, h].astype(F32), dev(dz=1))
                g = 1 - h
                got(b[g], land.at[3 + s, g])
                b[g] = send(4 + s, g, own(zo(-k), g) + land[3 + s, g].astype(F32), dev(dz=-1))
        yield
        for h in range(2):
            got(a[h], land.at[3, h])
            got(b[h], land.at[7, h])
            To[1, 2 * h:2 * h + 2, z] = (
                own(z, h) + land[3, h].astype(F32) + land[7, h].astype(F32)
            )
        order = (2, 1, 3)
        i = group()
        for d in order:
            sy[1][d - 1] = To[1, yo(d), z].astype(BF16)
            put(sy[1].at[d - 1], ly[1].at[d - 1], dev(dy=d), i)
        yield
        got(i, ly[1])
        v = To[1, y, z]
        for d in range(3):
            v = v + ly[1][d].astype(F32)
        fin[1] = v.reshape(2, 8, QC)

    t_in = {}
    sums = {1: sum_z_first(), 0: sum_y_first()}
    for core, j in ((sib, 1), (sib, 0), (c, 1), (c, 0)):
        w = pl.ds(pl.multiple_of((2 * core + j) * QC, QC), QC)
        t = dot(Dk[0], wk[w, :], 1, 1) + dot(Dv[0], wv[w, :], 1, 1)
        if core is sib:
            Ts[j] = t.astype(BF16).reshape(NY, NZ, 16, QC)
            t_in[j] = put(Ts.at[j], Tr.at[j], sibling)
        else:
            got(t_in[j], Tr.at[j])
            To[j] = t.reshape(NY, NZ, 16, QC) + Tr[j].astype(F32)
            next(sums[j])
        if j == 0:
            next(ea)
    next(xv)

    gsel = jnp.where(c == 0, gain[:, :hc], gain[:, hc:])
    for j in range(2):
        prod = To[j].reshape(ROWS, QC) * G[2 * c + j].reshape(ROWS, QC).astype(F32)
        terms = jnp.sum(prod, axis=0, keepdims=True) / gsel[:, j * QC:(j + 1) * QC]
        for r in range(4):
            gz[z, 4 * j + r:4 * j + r + 1, :] = terms[:, r * 256:(r + 1) * 256]

    def sum_gain():
        def spread(buf, me, to, n):
            i = group()
            for d in range(1, n):
                put(buf.at[me], buf.at[me], to(d), i)
            return i

        i = spread(gz, z, lambda d: dev(dz=d), NZ)
        yield
        got(i, gz.at[pl.ds(0, NZ - 1)])
        gy[y] = jnp.sum(gz[...], axis=0)
        i = spread(gy, y, lambda d: dev(dy=d), NY)
        yield
        got(i, gy.at[pl.ds(0, NY - 1)])
        gx[x] = jnp.sum(gy[...], axis=0)
        i = spread(gx, x, lambda d: dev(dx=d), NX)
        yield
        got(i, gx.at[pl.ds(0, NX - 1)])
        gf[c] = jnp.sum(gx[...], axis=0) / NX
        i = put(gf.at[c], gf.at[c], sibling)
        yield
        got(i, gf.at[sib])
        for h in range(2):
            for r in range(8):
                lo = h * hc + r * 256
                dg_ref[0:1, lo:lo + 256] = gf[h, r:r + 1, :]

    def weight_part(buf, total, out, k):
        for q in range(4):
            r = slice(q * EC, (q + 1) * EC)
            half = slice(q % 2 * EC, (q % 2 + 1) * EC)
            if k == 0:
                cols = G[x, :, :, :, r]
            else:
                cols = E[q // 2, k - 1, :, :, :, half]
            part = dot(cols.reshape(ROWS, EC), buf[k], 0, 0)
            if k == 0:
                total[r, :] = part
            elif k == 2:
                out[r, :] = ((total[r, :] + part) / NX).astype(BF16)
            else:
                total[r, :] += part

    background += [sums[1], sums[0]]
    gain_sum = sum_gain()
    poll()
    next(gain_sum)
    for h in range(2):
        cols = slice(h * HD, (h + 1) * HD)
        dq_ref[:, cols] = (dot(dsc[h], keys[:, cols], 0, 0) * scale).astype(BF16)
    weight_part(Dv, accv, dwv_ref, 0)
    poll()
    next(gain_sum)
    next(ea)
    weight_part(Dk, acck, dwk_ref, 0)
    poll()
    next(gain_sum)
    next(ea, None)
    next(xv)
    poll()
    got(e_over, E.at[sib])
    weight_part(Dv, accv, dwv_ref, 1)
    weight_part(Dv, accv, dwv_ref, 3)
    next(xk)
    poll()
    next(xv, None)
    weight_part(Dv, accv, dwv_ref, 2)
    poll()
    next(gain_sum)
    drain()

    i = put(fin.at[:, sib], dn, sibling)
    next(xk)
    weight_part(Dk, acck, dwk_ref, 1)
    weight_part(Dk, acck, dwk_ref, 3)
    got(i, dn)
    own_half = jnp.concatenate([fin[0, c], fin[1, c]], axis=1)
    other_half = jnp.concatenate([dn[0], dn[1]], axis=1)
    dnorm = jnp.concatenate(
        [jnp.where(c == 0, own_half, other_half), jnp.where(c == 0, other_half, own_half)],
        axis=1,
    )
    scaled = gain * dnorm
    hg = (scaled - xhat * jnp.mean(scaled * xhat, axis=-1, keepdims=True)) / rms
    hg_ref[...] = hg.astype(BF16)
    next(gain_sum, None)
    next(xk, None)
    weight_part(Dk, acck, dwk_ref, 2)
    for cp in sends.values():
        cp.wait_send()
    each_cols(lambda cp: cp.wait_send())
    for d in range(NZ):
        @pl.when(d != z)
        def _():
            slab_to(d).wait_send()
    assert count[0] == NSEM, count[0]


def place(dq, dwk, dwv, hg, dg, dq_out, dwk_out, dwv_out, hg_out, dg_out, sem):
    copies = []
    for src, dst in ((dwk, dwk_out), (dwv, dwv_out), (dq, dq_out)):
        step = src.shape[0] // 4
        for p in range(4):
            rows = pl.ds(p * step, step)
            cp = pltpu.make_async_copy(src.at[rows], dst.at[rows], sem.at[len(copies)])
            cp.start()
            copies.append(cp)
    hg_out[...] = hg[...]
    dg_out[...] = dg[...]
    for cp in copies:
        cp.wait()


def local(enc_hidden, enc_gain, key_weight, value_weight, queries, cotangent, enc_len, dec_len):
    vmem = pl.BlockSpec(memory_space=pltpu.VMEM)
    hbm = pl.BlockSpec(memory_space=pl.ANY)
    v = pltpu.VMEM
    shapes = (
        jax.ShapeDtypeStruct((DEC, WID), BF16),
        jax.ShapeDtypeStruct((QC, WID), BF16),
        jax.ShapeDtypeStruct((QC, WID), BF16),
        jax.ShapeDtypeStruct((8, D), BF16),
        jax.ShapeDtypeStruct((1, D), F32),
    )
    outs = pl.pallas_call(
        kernel,
        out_shape=tuple(v(o.shape, o.dtype) for o in shapes),
        in_specs=[vmem, vmem, hbm, hbm, vmem, vmem, hbm, hbm],
        out_specs=(vmem,) * 5,
        scratch_shapes=[
            v((D, WID), BF16),
            v((D, WID), BF16),
            pltpu.SemaphoreType.DMA((4,)),
            pltpu.SMEM((1,), jnp.int32),
            pltpu.SMEM((1,), jnp.int32),
            v((8, D), F32),
            v((8, D // 2), F32),
            v((4, NY, NZ, 16, QC), BF16),
            v((2, 3, NY, NZ, 16, HC), BF16),
            v((ROWS, WID), F32),
            v((ROWS, WID), BF16),
            v((ROWS, WID), BF16),
            v((2, ROWS, DEC), F32),
            v((DEC, WID), BF16),
            v((2, ROWS, DEC), BF16),
            v((4, ROWS, WID), BF16),
            v((4, ROWS, WID), BF16),
            v((2, NY, NZ, 16, QC), BF16),
            v((2, NY, NZ, 16, QC), BF16),
            v((2, NY, NZ, 16, QC), F32),
            [v((3, NZ, 16, QC), BF16), v((3, 16, QC), BF16)],
            [v((NZ, 16, QC), BF16), v((8, 2, 2, 16, QC), BF16)],
            [v((3, NZ, 16, QC), BF16), v((3, 16, QC), BF16)],
            [v((NZ, 16, QC), BF16), v((8, 2, 2, 16, QC), BF16)],
            v((2, 2, 8, QC), F32),
            v((2, 8, QC), F32),
            v((QC, WID), F32),
            v((QC, WID), F32),
            v((NZ, 8, 256), F32),
            v((NY, 8, 256), F32),
            v((NX, 8, 256), F32),
            v((2, 8, 256), F32),
            pltpu.SemaphoreType.DMA((NSEND,)),
            pltpu.SemaphoreType.DMA((NSEM,)),
            pltpu.SemaphoreType.DMA((4,)),
            pltpu.SemaphoreType.DMA((3,)),
            pltpu.SemaphoreType.DMA((NZ + 1,)),
        ],
        compiler_params=pltpu.CompilerParams(
            collective_id=0, has_side_effects=True, vmem_limit_bytes=52 * 1024 * 1024
        ),
        cost_estimate=pl.CostEstimate(
            flops=15_000_000_000, bytes_accessed=12_000_000, transcendentals=300_000
        ),
    )(
        enc_hidden[0], enc_gain, key_weight[0, 0], value_weight[0, 0],
        queries[0, 0], cotangent[0, 0], enc_len, dec_len,
    )
    dq, dwk, dwv, hg, dg = pl.pallas_call(
        place,
        out_shape=shapes,
        in_specs=[vmem] * 5,
        out_specs=(hbm, hbm, hbm, vmem, vmem),
        scratch_shapes=[pltpu.SemaphoreType.DMA((12,))],
    )(*[pltpu.with_memory_space_constraint(o, pltpu.VMEM) for o in outs])
    return dq[None, None], dwk[None], dwv[None], hg[None], dg[0]


def solution(mesh):
    placed = (
        P("replica", ("section", "tensor"), None),
        P("replica", None),
        P("replica", "section", None, "tensor"),
        P("replica", "section", None, "tensor"),
        P("replica", "section", None, "tensor"),
        P("replica", "section", None, "tensor"),
        P("replica"),
        P("replica"),
    )
    return jax.shard_map(
        local,
        mesh=mesh,
        in_specs=placed,
        out_specs=(
            P("replica", "section", None, "tensor"),
            P("section", "replica", "tensor"),
            P("section", "replica", "tensor"),
            P("replica", ("section", "tensor"), None),
            P(),
        ),
        check_vma=False,
    )
```

```python
import jax
import jax.numpy as jnp
from jax import lax
from jax.experimental import pallas as pl
from jax.experimental.pallas import tpu as pltpu
from jax.sharding import PartitionSpec as P

MESH = pl.DeviceIdType.MESH
F32 = jnp.float32
BF16 = jnp.bfloat16
D = 4096
ROWS = 512
DEC = 256
HD = 256
WID = 512
NX, NY, NZ = 4, 4, 8
QC = D // 4
HC = QC // 2
EC = QC // 4
NSEM = 89
NSEND = 112


def dot(a, b, ca=1, cb=0):
    return lax.dot_general(a, b, (((ca,), (cb,)), ((), ())), preferred_element_type=F32)


def kernel(
    hid_ref, gain_ref, kw_ref, vw_ref, q_ref, ct_ref, elen_hbm, dlen_hbm,
    dq_ref, dwk_ref, dwv_ref, hg_ref, dg_ref,
    wk, wv, wsem, elen_ref, dlen_ref, n32, x32, G, E, acc, keys, vals, probs, grad, dsc, Dv, Dk,
    Ts, Tr, To, ly, lz, sy, sz, fin, dn, accv, acck,
    gz, gy, gx, gf, ssem, rsem, esend, erecv, zsem,
):
    x = lax.axis_index("replica")
    sec = lax.axis_index("section")
    zlo = lax.axis_index("tensor")
    c = lax.rem(sec, 2)
    y = lax.rem(lax.div(sec, 2), NY)
    z = lax.div(sec, 2 * NY) * 4 + zlo
    sib = 1 - c

    def dev(dx=0, dy=0, dz=0, core=None):
        xx = lax.rem(x + dx + NX, NX)
        yy = lax.rem(y + dy + NY, NY)
        zz = lax.rem(z + dz + NZ, NZ)
        cc = c if core is None else core
        return (xx, (lax.div(zz, 4) * NY + yy) * 2 + cc, lax.rem(zz, 4))

    def xo(d):
        return lax.rem(x + d + NX, NX)

    def yo(d):
        return lax.rem(y + d + NY, NY)

    def zo(d):
        return lax.rem(z + d + NZ, NZ)

    sibling = dev(core=sib)
    count = [0]
    order = [0]
    sends = {}

    def group():
        count[0] += 1
        return count[0] - 1

    def put(src, dst, to, i=None):
        i = group() if i is None else i
        s = order[0] % NSEND
        order[0] += 1
        if s in sends:
            sends[s].wait_send()
        cp = pltpu.make_async_remote_copy(
            src_ref=src, dst_ref=dst, send_sem=ssem.at[s], recv_sem=rsem.at[i],
            device_id=to, device_id_type=MESH,
        )
        cp.start()
        sends[s] = cp
        return i

    def got(i, region):
        pltpu.make_async_remote_copy(
            src_ref=region, dst_ref=region, send_sem=ssem.at[0], recv_sem=rsem.at[i],
            device_id=sibling, device_id_type=MESH,
        ).wait_recv()

    background = []

    def poll(n=1):
        for _ in range(n):
            for g in list(background):
                if next(g, "end") == "end":
                    background.remove(g)

    def drain():
        while background:
            poll()

    wcopies = [
        pltpu.make_async_copy(kw_ref, wk, wsem.at[0]),
        pltpu.make_async_copy(vw_ref, wv, wsem.at[1]),
        pltpu.make_async_copy(elen_hbm, elen_ref, wsem.at[2]),
        pltpu.make_async_copy(dlen_hbm, dlen_ref, wsem.at[3]),
    ]
    for w in wcopies:
        w.start()

    partners = [sibling]
    partners += [dev(dz=d) for d in range(1, NZ)]
    partners += [dev(dy=d) for d in range(1, NY)]
    partners += [dev(dx=d, core=e) for d in range(1, NX) for e in (c, sib)]
    barrier = pltpu.get_barrier_semaphore()
    for p in partners:
        pl.semaphore_signal(barrier, inc=1, device_id=p, device_id_type=MESH)

    hid = hid_ref[...].astype(F32)
    gain = gain_ref[...].astype(F32)
    rms = jnp.sqrt(jnp.mean(hid * hid, axis=-1, keepdims=True) + 1e-06)
    xhat = hid / rms
    n32[...] = (xhat * gain).astype(BF16).astype(F32)
    pl.semaphore_wait(barrier, len(partners))

    hc = D // 2
    i = put(n32.at[:, pl.ds(pl.multiple_of(sib * hc, hc), hc)], x32, sibling)
    mine = jnp.where(c == 0, n32[:, :hc], n32[:, hc:])
    got(i, x32)
    other = x32[...]
    chip = jnp.concatenate(
        [jnp.where(c == 0, mine, other), jnp.where(c == 0, other, mine)], axis=0
    ).astype(BF16)
    for j in range(2):
        G[2 * c + j, y, z] = chip[:, j * QC:(j + 1) * QC]

    def cols_to(j, half):
        q = 2 * c + j
        slot = jnp.maximum(lax.rem(x - q + NX, NX) - 1, 0)
        return pltpu.make_async_remote_copy(
            src_ref=G.at[q, y, z, :, pl.ds(half * HC, HC)], dst_ref=E.at[half, slot, y, z],
            send_sem=esend.at[2 * j + half], recv_sem=erecv.at[slot],
            device_id=dev(dx=q - x, core=half), device_id_type=MESH,
        )

    def each_cols(act):
        for j in range(2):
            @pl.when(2 * c + j != x)
            def _():
                for half in range(2):
                    act(cols_to(j, half))

    ydist = (1, 3, 2)

    def plane_gather(slab_a, half_a, slab_b, chunk_b, over_a, over_b, some_a, some_b, over):
        def forward(region):
            put(region(c), region(c), sibling, over)

        def along_y(slab, zz, i):
            for d in ydist:
                put(slab(y, zz), slab(y, zz), dev(dy=d), i)

        b_y = group()
        along_y(slab_b, z, b_y)
        a_z = {d: put(slab_a(y, z), slab_a(y, z), dev(dz=d)) for d in (1, 7, 2, 6, 3, 5, 4)}
        a_y = {e: group() for e in (0, 2, 3)}
        group_of = {0: 0, 1: 0, 7: 0, 2: 2, 6: 2, 3: 3, 5: 3, 4: 3}
        along_y(slab_a, z, a_y[0])

        def from_z(*dist):
            for d in dist:
                zz = zo(-d)
                got(a_z[d], slab_a(y, zz))
                along_y(slab_a, zz, a_y[group_of[d]])

        def from_y(e, n):
            got(a_y[e], some_a(n))

        yield
        from_z(1, 7)
        got(b_y, some_b())
        right = {h: put(chunk_b(z, h), chunk_b(z, h), dev(dz=1)) for h in (0, 1)}
        left = {h: put(chunk_b(z, h), chunk_b(z, h), dev(dz=-1)) for h in (1, 0)}
        forward(lambda cc: over_b(cc, z))

        def hop(k):
            for h in (0, 1):
                zr, zl = zo(-k), zo(k)
                if k < 4 or h == 0:
                    got(right[h], chunk_b(zr, h))
                    if k < 3 or (k == 3 and h == 0):
                        right[h] = put(chunk_b(zr, h), chunk_b(zr, h), dev(dz=1))
                g = 1 - h
                if k < 4 or g == 1:
                    got(left[g], chunk_b(zl, g))
                    if k < 3 or (k == 3 and g == 1):
                        left[g] = put(chunk_b(zl, g), chunk_b(zl, g), dev(dz=-1))
            forward(lambda cc: over_b(cc, zo(-k)))
            if k < 4:
                forward(lambda cc: over_b(cc, zo(k)))

        from_z(2, 6, 3, 5)
        yield
        hop(1)
        from_z(4)
        forward(lambda cc: over_a(cc, y))
        yield
        from_y(0, 3)
        hop(2)
        yield
        from_y(2, 2)
        hop(3)
        yield
        from_y(3, 3)
        for d in ydist:
            yy = yo(-d)
            forward(lambda cc: over_a(cc, yy))
        yield
        hop(4)

    g_over, e_over = group(), group()
    ga = plane_gather(
        lambda yy, zz: G.at[2 * c, yy, zz],
        lambda yy, zz, h: G.at[2 * c, yy, zz, :, pl.ds(h * HC, HC)],
        lambda yy, zz: G.at[2 * c + 1, yy, zz],
        lambda zz, h: G.at[2 * c + 1, pl.ds(2 * h, 2), zz],
        lambda cc, yy: G.at[2 * cc, yy],
        lambda cc, zz: G.at[2 * cc + 1, :, zz],
        lambda n: G.at[2 * c, pl.ds(0, 3), pl.ds(0, n)],
        lambda: G.at[2 * c + 1, pl.ds(0, 3), z],
        g_over,
    )
    next(ga)
    each_cols(lambda cp: cp.start())
    for _ in range(5):
        next(ga)
    wcopies[0].wait()
    acc[...] = dot(
        G[2 * c].reshape(ROWS, QC), wk[pl.ds(pl.multiple_of(2 * c * QC, QC), QC), :]
    )
    for _ in ga:
        pass

    lo, hi = pl.ds(0, EC), pl.ds(EC, EC)
    every = slice(None)
    ea = plane_gather(
        lambda yy, zz: E.at[c, :, yy, zz, :, lo],
        lambda yy, zz, h: E.at[c, :, yy, zz, :, pl.ds(h * (EC // 2), EC // 2)],
        lambda yy, zz: E.at[c, :, yy, zz, :, hi],
        lambda zz, h: E.at[c, :, pl.ds(2 * h, 2), zz, :, hi],
        lambda cc, yy: E.at[cc, :, yy, :, :, lo],
        lambda cc, zz: E.at[cc, :, :, zz, :, hi],
        lambda n: E.at[c, :, pl.ds(0, 3), pl.ds(0, n), :, lo],
        lambda: E.at[c, :, pl.ds(0, 3), z, :, hi],
        e_over,
    )
    for k in range(3):
        slab = E.at[c, k, y, z]
        pltpu.make_async_remote_copy(
            src_ref=slab, dst_ref=slab, send_sem=esend.at[0], recv_sem=erecv.at[k],
            device_id=sibling, device_id_type=MESH,
        ).wait_recv()
    next(ea)

    def project(w, out, first):
        for j in range(1 if first else 0, 4):
            if first and j == 2:
                got(g_over, G.at[pl.ds(2 * sib, 2)])
            q = lax.rem(2 * c + j, 4)
            part = dot(G[q].reshape(ROWS, QC), w[pl.ds(pl.multiple_of(q * QC, QC), QC), :])
            if j == 0:
                acc[...] = part
            elif j < 3:
                acc[...] += part
            else:
                out[...] = (acc[...] + part).astype(BF16)

    scale = HD ** (-0.5)
    row = lax.broadcasted_iota(jnp.int32, (ROWS, 1), 0)
    inner = row & 7
    row_c = (row >> 3) & 1
    row_z = (row >> 4) & 7
    row_y = row >> 7
    pos = ((((row_z >> 2) * NY + row_y) * 2 + row_c) * 4 + (row_z & 3)) * 8 + inner
    wcopies[2].wait()
    wcopies[3].wait()
    keep = pos < elen_ref[0]
    live = lax.broadcasted_iota(jnp.int32, (DEC, 1), 0) < dlen_ref[0]
    grad[...] = jnp.where(live, ct_ref[...], jnp.zeros((DEC, WID), BF16))
    project(wk, keys, True)
    for h in range(2):
        cols = slice(h * HD, (h + 1) * HD)
        s = dot(keys[:, cols], q_ref[:, cols], 1, 1) * scale
        s = jnp.where(keep, s, -1e30)
        top = jnp.max(s, axis=0, keepdims=True)
        e = jnp.where(keep, jnp.exp(s - top), 0.0)
        p = e / jnp.sum(e, axis=0, keepdims=True)
        probs[h] = p
        Dv[0, :, cols] = dot(p.astype(BF16), grad[:, cols]).astype(BF16)

    def along_x(buf):
        def at(slot, h):
            return buf.at[slot, pl.ds(h * (ROWS // 2), ROWS // 2)]

        a0 = put(at(0, 0), at(3, 0), dev(dx=1))
        b1 = put(at(0, 1), at(1, 1), dev(dx=-1))
        a1 = put(at(0, 1), at(3, 1), dev(dx=1))
        b0 = put(at(0, 0), at(1, 0), dev(dx=-1))
        yield
        got(a0, at(3, 0))
        f0 = put(at(3, 0), at(2, 0), dev(dx=1))
        got(b1, at(1, 1))
        f1 = put(at(1, 1), at(2, 1), dev(dx=-1))
        yield
        got(a1, at(3, 1))
        got(b0, at(1, 0))
        yield
        got(f0, at(2, 0))
        got(f1, at(2, 1))

    xv = along_x(Dv)
    next(xv)
    wcopies[1].wait()
    project(wv, vals, False)
    next(ea)
    for h in range(2):
        cols = slice(h * HD, (h + 1) * HD)
        dp = dot(vals[:, cols], grad[:, cols], 1, 1)
        p = probs[h]
        ds = (p * (dp - jnp.sum(p * dp, axis=0, keepdims=True))).astype(BF16)
        dsc[h] = ds
        Dk[0, :, cols] = (dot(ds, q_ref[:, cols]) * scale).astype(BF16)
    xk = along_x(Dk)
    next(xk)

    def slab_to(zz):
        to = (x, (zz // 4 * NY + y) * 2 + c, zz % 4)
        return pltpu.make_async_remote_copy(
            src_ref=sz[0].at[zz], dst_ref=lz[0].at[z], send_sem=zsem.at[zz],
            recv_sem=zsem.at[NZ], device_id=to, device_id_type=MESH,
        )

    def sum_y_first():
        order = (2, 1, 3)
        idx = [group(), group()]
        for h in range(2):
            zs = pl.ds(4 * h, 4)
            for d in order:
                sy[0][d - 1, zs] = To[0, yo(d), zs].astype(BF16)
                put(sy[0].at[d - 1, zs], ly[0].at[d - 1, zs], dev(dy=d), idx[h])
        lz[0][z] = jnp.zeros((16, QC), BF16)
        yield
        for h in range(2):
            yield
            zs = pl.ds(4 * h, 4)
            got(idx[h], ly[0].at[:, zs])
            v = To[0, y, zs]
            for d in range(3):
                v = v + ly[0][d, zs].astype(F32)
            To[0, y, zs] = v
            sz[0][zs] = v.astype(BF16)
            for zz in range(4 * h, 4 * h + 4):
                @pl.when(zz != z)
                def _():
                    slab_to(zz).start()
        yield
        yield
        got_all = lz[0].at[pl.ds(0, 7)]
        pltpu.make_async_remote_copy(
            src_ref=got_all, dst_ref=got_all, send_sem=zsem.at[0], recv_sem=zsem.at[NZ],
            device_id=sibling, device_id_type=MESH,
        ).wait_recv()
        v = To[0, y, z]
        for d in range(NZ):
            v = v + lz[0][d].astype(F32)
        fin[0] = v.reshape(2, 8, QC)

    def sum_z_first():
        stage, land = sz[1], lz[1]

        def own(zz, h):
            return To[1, 2 * h:2 * h + 2, zz]

        def send(slot, h, value, to):
            stage[slot, h] = value.astype(BF16)
            return put(stage.at[slot, h], land.at[slot, h], to)

        a, b = [None, None], [None, None]
        a[0] = send(0, 0, own(zo(4), 0), dev(dz=1))
        b[1] = send(4, 1, own(zo(4), 1), dev(dz=-1))
        a[1] = send(1, 1, own(zo(3), 1), dev(dz=1))
        b[0] = send(5, 0, own(zo(-3), 0), dev(dz=-1))
        for s, k in ((1, 3), (2, 2), (3, 1)):
            yield
            for h in ((0, 1) if s > 1 else (0,)):
                got(a[h], land.at[s - 1, h])
                a[h] = send(s, h, own(zo(k), h) + land[s - 1, h].astype(F32), dev(dz=1))
                g = 1 - h
                got(b[g], land.at[3 + s, g])
                b[g] = send(4 + s, g, own(zo(-k), g) + land[3 + s, g].astype(F32), dev(dz=-1))
        yield
        for h in range(2):
            got(a[h], land.at[3, h])
            got(b[h], land.at[7, h])
            To[1, 2 * h:2 * h + 2, z] = (
                own(z, h) + land[3, h].astype(F32) + land[7, h].astype(F32)
            )
        order = (2, 1, 3)
        i = group()
        for d in order:
            sy[1][d - 1] = To[1, yo(d), z].astype(BF16)
            put(sy[1].at[d - 1], ly[1].at[d - 1], dev(dy=d), i)
        yield
        got(i, ly[1])
        v = To[1, y, z]
        for d in range(3):
            v = v + ly[1][d].astype(F32)
        fin[1] = v.reshape(2, 8, QC)

    t_in = {}
    sums = {1: sum_z_first(), 0: sum_y_first()}
    for core, j in ((sib, 1), (sib, 0), (c, 1), (c, 0)):
        w = pl.ds(pl.multiple_of((2 * core + j) * QC, QC), QC)
        t = dot(Dk[0], wk[w, :], 1, 1) + dot(Dv[0], wv[w, :], 1, 1)
        if core is sib:
            Ts[j] = t.astype(BF16).reshape(NY, NZ, 16, QC)
            t_in[j] = put(Ts.at[j], Tr.at[j], sibling)
        else:
            got(t_in[j], Tr.at[j])
            To[j] = t.reshape(NY, NZ, 16, QC) + Tr[j].astype(F32)
            next(sums[j])
        if j == 0:
            next(ea)
    next(xv)

    gsel = jnp.where(c == 0, gain[:, :hc], gain[:, hc:])
    for j in range(2):
        prod = To[j].reshape(ROWS, QC) * G[2 * c + j].reshape(ROWS, QC).astype(F32)
        terms = jnp.sum(prod, axis=0, keepdims=True) / gsel[:, j * QC:(j + 1) * QC]
        for r in range(4):
            gz[z, 4 * j + r:4 * j + r + 1, :] = terms[:, r * 256:(r + 1) * 256]

    def sum_gain():
        def spread(buf, me, to, n):
            i = group()
            for d in range(1, n):
                put(buf.at[me], buf.at[me], to(d), i)
            return i

        i = spread(gz, z, lambda d: dev(dz=d), NZ)
        yield
        got(i, gz.at[pl.ds(0, NZ - 1)])
        gy[y] = jnp.sum(gz[...], axis=0)
        i = spread(gy, y, lambda d: dev(dy=d), NY)
        yield
        got(i, gy.at[pl.ds(0, NY - 1)])
        gx[x] = jnp.sum(gy[...], axis=0)
        i = spread(gx, x, lambda d: dev(dx=d), NX)
        yield
        got(i, gx.at[pl.ds(0, NX - 1)])
        gf[c] = jnp.sum(gx[...], axis=0) / NX
        i = put(gf.at[c], gf.at[c], sibling)
        yield
        got(i, gf.at[sib])
        for h in range(2):
            for r in range(8):
                lo = h * hc + r * 256
                dg_ref[0:1, lo:lo + 256] = gf[h, r:r + 1, :]

    def weight_part(buf, total, out, k):
        for q in range(4):
            r = slice(q * EC, (q + 1) * EC)
            half = slice(q % 2 * EC, (q % 2 + 1) * EC)
            if k == 0:
                cols = G[x, :, :, :, r]
            else:
                cols = E[q // 2, k - 1, :, :, :, half]
            part = dot(cols.reshape(ROWS, EC), buf[k], 0, 0)
            if k == 0:
                total[r, :] = part
            elif k == 2:
                out[r, :] = ((total[r, :] + part) / NX).astype(BF16)
            else:
                total[r, :] += part

    background += [sums[1], sums[0]]
    gain_sum = sum_gain()
    poll()
    next(gain_sum)
    for h in range(2):
        cols = slice(h * HD, (h + 1) * HD)
        dq_ref[:, cols] = (dot(dsc[h], keys[:, cols], 0, 0) * scale).astype(BF16)
    weight_part(Dv, accv, dwv_ref, 0)
    poll()
    next(gain_sum)
    next(ea)
    weight_part(Dk, acck, dwk_ref, 0)
    poll()
    next(gain_sum)
    for _ in ea:
        pass
    next(xv)
    poll()
    got(e_over, E.at[sib])
    weight_part(Dv, accv, dwv_ref, 1)
    weight_part(Dv, accv, dwv_ref, 3)
    next(xk)
    poll()
    next(xv, None)
    weight_part(Dv, accv, dwv_ref, 2)
    poll()
    next(gain_sum)
    drain()

    i = put(fin.at[:, sib], dn, sibling)
    next(xk)
    weight_part(Dk, acck, dwk_ref, 1)
    weight_part(Dk, acck, dwk_ref, 3)
    got(i, dn)
    own_half = jnp.concatenate([fin[0, c], fin[1, c]], axis=1)
    other_half = jnp.concatenate([dn[0], dn[1]], axis=1)
    dnorm = jnp.concatenate(
        [jnp.where(c == 0, own_half, other_half), jnp.where(c == 0, other_half, own_half)],
        axis=1,
    )
    scaled = gain * dnorm
    hg = (scaled - xhat * jnp.mean(scaled * xhat, axis=-1, keepdims=True)) / rms
    hg_ref[...] = hg.astype(BF16)
    next(gain_sum, None)
    next(xk, None)
    weight_part(Dk, acck, dwk_ref, 2)
    for cp in sends.values():
        cp.wait_send()
    each_cols(lambda cp: cp.wait_send())
    for d in range(NZ):
        @pl.when(d != z)
        def _():
            slab_to(d).wait_send()
    assert count[0] == NSEM, count[0]


def place(dq, dwk, dwv, hg, dg, dq_out, dwk_out, dwv_out, hg_out, dg_out, sem):
    copies = []
    for src, dst in ((dwk, dwk_out), (dwv, dwv_out), (dq, dq_out)):
        step = src.shape[0] // 4
        for p in range(4):
            rows = pl.ds(p * step, step)
            cp = pltpu.make_async_copy(src.at[rows], dst.at[rows], sem.at[len(copies)])
            cp.start()
            copies.append(cp)
    hg_out[...] = hg[...]
    dg_out[...] = dg[...]
    for cp in copies:
        cp.wait()


def local(enc_hidden, enc_gain, key_weight, value_weight, queries, cotangent, enc_len, dec_len):
    vmem = pl.BlockSpec(memory_space=pltpu.VMEM)
    hbm = pl.BlockSpec(memory_space=pl.ANY)
    v = pltpu.VMEM
    shapes = (
        jax.ShapeDtypeStruct((DEC, WID), BF16),
        jax.ShapeDtypeStruct((QC, WID), BF16),
        jax.ShapeDtypeStruct((QC, WID), BF16),
        jax.ShapeDtypeStruct((8, D), BF16),
        jax.ShapeDtypeStruct((1, D), F32),
    )
    outs = pl.pallas_call(
        kernel,
        out_shape=tuple(v(o.shape, o.dtype) for o in shapes),
        in_specs=[vmem, vmem, hbm, hbm, vmem, vmem, hbm, hbm],
        out_specs=(vmem,) * 5,
        scratch_shapes=[
            v((D, WID), BF16),
            v((D, WID), BF16),
            pltpu.SemaphoreType.DMA((4,)),
            pltpu.SMEM((1,), jnp.int32),
            pltpu.SMEM((1,), jnp.int32),
            v((8, D), F32),
            v((8, D // 2), F32),
            v((4, NY, NZ, 16, QC), BF16),
            v((2, 3, NY, NZ, 16, HC), BF16),
            v((ROWS, WID), F32),
            v((ROWS, WID), BF16),
            v((ROWS, WID), BF16),
            v((2, ROWS, DEC), F32),
            v((DEC, WID), BF16),
            v((2, ROWS, DEC), BF16),
            v((4, ROWS, WID), BF16),
            v((4, ROWS, WID), BF16),
            v((2, NY, NZ, 16, QC), BF16),
            v((2, NY, NZ, 16, QC), BF16),
            v((2, NY, NZ, 16, QC), F32),
            [v((3, NZ, 16, QC), BF16), v((3, 16, QC), BF16)],
            [v((NZ, 16, QC), BF16), v((8, 2, 2, 16, QC), BF16)],
            [v((3, NZ, 16, QC), BF16), v((3, 16, QC), BF16)],
            [v((NZ, 16, QC), BF16), v((8, 2, 2, 16, QC), BF16)],
            v((2, 2, 8, QC), F32),
            v((2, 8, QC), F32),
            v((QC, WID), F32),
            v((QC, WID), F32),
            v((NZ, 8, 256), F32),
            v((NY, 8, 256), F32),
            v((NX, 8, 256), F32),
            v((2, 8, 256), F32),
            pltpu.SemaphoreType.DMA((NSEND,)),
            pltpu.SemaphoreType.DMA((NSEM,)),
            pltpu.SemaphoreType.DMA((4,)),
            pltpu.SemaphoreType.DMA((3,)),
            pltpu.SemaphoreType.DMA((NZ + 1,)),
        ],
        compiler_params=pltpu.CompilerParams(
            collective_id=0, has_side_effects=True, vmem_limit_bytes=52 * 1024 * 1024
        ),
        cost_estimate=pl.CostEstimate(
            flops=15_000_000_000, bytes_accessed=12_000_000, transcendentals=300_000
        ),
    )(
        enc_hidden[0], enc_gain, key_weight[0, 0], value_weight[0, 0],
        queries[0, 0], cotangent[0, 0], enc_len, dec_len,
    )
    dq, dwk, dwv, hg, dg = pl.pallas_call(
        place,
        out_shape=shapes,
        in_specs=[vmem] * 5,
        out_specs=(hbm, hbm, hbm, vmem, vmem),
        scratch_shapes=[pltpu.SemaphoreType.DMA((12,))],
    )(*[pltpu.with_memory_space_constraint(o, pltpu.VMEM) for o in outs])
    return dq[None, None], dwk[None], dwv[None], hg[None], dg[0]


def solution(mesh):
    placed = (
        P("replica", ("section", "tensor"), None),
        P("replica", None),
        P("replica", "section", None, "tensor"),
        P("replica", "section", None, "tensor"),
        P("replica", "section", None, "tensor"),
        P("replica", "section", None, "tensor"),
        P("replica"),
        P("replica"),
    )
    return jax.shard_map(
        local,
        mesh=mesh,
        in_specs=placed,
        out_specs=(
            P("replica", "section", None, "tensor"),
            P("section", "replica", "tensor"),
            P("section", "replica", "tensor"),
            P("replica", ("section", "tensor"), None),
            P(),
        ),
        check_vma=False,
    )
```
